128 devices in a mesh: ctx: 16 (over y, x), exp: 8 (over z, core).
Axes of the slice: x: 4, y: 4, z: 4, core: 2. Of those that a mesh axis runs over, the one named last changes fastest.
Arguments:
- tokens: bfloat16 [1024, 7168], P('exp', 'ctx'), may hold values from -6 to 6
- expert_ids: int32 [1024, 8], P('exp'), may hold values from 0 to 15, as said below
- route_weights: float32 [1024, 8], P('exp'), may hold values from 0.05 to 0.5
- output_grad: bfloat16 [1024, 7168], P('exp', 'ctx'), may hold values from -6 to 6
- w_gate: bfloat16 [16, 7168, 2048], P('exp', 'ctx'), may hold values from -0.0625 to 0.0625
- w_up: bfloat16 [16, 7168, 2048], P('exp', 'ctx'), may hold values from -0.0625 to 0.0625
- w_down: bfloat16 [16, 2048, 7168], P('exp', None, 'ctx'), may hold values from -0.125 to 0.125
Outputs:
- mixed: bfloat16 [1024, 7168], P('exp', 'ctx')
- token_grad: bfloat16 [1024, 7168], P('exp', 'ctx')
- weight_grad: float32 [1024, 8], P('exp')
- gate_grad: bfloat16 [16, 7168, 2048], P('exp', 'ctx')
- up_grad: bfloat16 [16, 7168, 2048], P('exp', 'ctx')
- down_grad: bfloat16 [16, 2048, 7168], P('exp', None, 'ctx')
The draws below stay inside these ranges and needn't reach their ends.
Inputs may be any that keep to these rules, and one draw needn't show every extreme that they name: `expert_ids`: each row names 8 different experts. In each aligned block of 128 rows (the rows of one index of exp) no expert is named by more than 96 rows, and one expert, the same in every block, is named by exactly 96 rows.
All inputs are finite; a program needn't handle non-finite values.
Results may differ from the reference program's by a relative error of at most 0.029.
Values may be sent and summed in bfloat16 or wider, within the bound.
No kernel may reach another device: no remote copies, remote signals or barrier semaphores. Data moves between devices by JAX's collectives and lax.ppermute only.
A program may use at most 192 MiB of HBM per device.

```python
import math
import jax
import jax.numpy as jnp
from jax import lax

D = 7168
HID = 2048
TOP = 8
EXPERTS = 16
TOK_E = 128
CAP = 96
TOKENS = 1024
FEAT = 448
N_CTX = 16


def draw_expert_ids(key, part):
    key = jax.random.fold_in(key, 7)
    first_key, second_key = jax.random.split(key)
    hottest = jax.random.randint(first_key, (), 0, EXPERTS)
    block_keys = jax.random.split(second_key, TOKENS // TOK_E)

    def draw_block(block_key):
        ranking_key, others_key, starts_key = jax.random.split(block_key, 3)
        ranking = jax.random.permutation(ranking_key, TOK_E)
        others = jax.random.permutation(others_key, EXPERTS - 1)
        starts = jax.random.permutation(starts_key, TOK_E) % (EXPERTS - 1)
        column = jnp.arange(TOP)
        placed = (starts[:, None] + column[None, :]) % (EXPERTS - 1)
        picked = others[placed]
        picked = picked + (picked >= hottest).astype(jnp.int32)
        takes_hottest = (ranking < CAP)[:, None] & (column == TOP - 1)[None, :]
        return jnp.where(takes_hottest, hottest, picked).astype(jnp.int32)
    return jax.vmap(draw_block)(block_keys).reshape(TOKENS, TOP)


def block_levels(stream_key, extent, shards, low, top_value):
    def one(position, shards_of):
        draws = jax.random.uniform(jax.random.fold_in(jax.random.fold_in(stream_key, 6), position), (shards_of,), jnp.float32, low / len(shards), top_value / len(shards))
        return jnp.repeat(jnp.exp(draws), extent[position] // shards_of).reshape((-1,) + (1,) * (len(extent) - position - 1))

    factor_of = one(*shards[0])
    for cut in shards[1:]:
        factor_of = factor_of * one(*cut)
    return factor_of


def normal_values(rng, extent, scale, limit, shards=(), kind=jnp.bfloat16):
    factor_of = block_levels(rng, extent, shards, -0.22, 0.18) if shards else 1.0
    drawn = jax.random.normal(rng, extent, jnp.float32) * scale * factor_of
    return jnp.minimum(jnp.maximum(drawn, -limit), limit).astype(kind)


def setup_inputs(seed: int = 0) -> dict:
    key_of = jax.random.split(jax.random.key(seed), 8)
    return {
        "tokens": normal_values(key_of[0], (TOKENS, D), 1.0, 6.0, ((0, 8), (1, 16))),
        "expert_ids": draw_expert_ids(jax.random.fold_in(key_of[7], 71), 0),
        "route_weights": jnp.clip(jnp.exp(math.log(0.5) - 2.3025851 * jax.random.uniform(key_of[2], (TOKENS, TOP), jnp.float32) ** block_levels(key_of[2], (TOKENS, TOP), ((0, 8),), -0.2, 0.2)), 0.05, 0.5),
        "output_grad": normal_values(key_of[3], (TOKENS, D), 1.0, 6.0, ((0, 8), (1, 16))),
        "w_gate": normal_values(key_of[4], (EXPERTS, D, HID), D ** -0.5, 0.0625, ((0, 8), (1, 16))),
        "w_up": normal_values(key_of[5], (EXPERTS, D, HID), D ** -0.5, 0.0625, ((0, 8), (1, 16))),
        "w_down": normal_values(key_of[6], (EXPERTS, HID, D), HID ** -0.5, 0.125, ((0, 8), (2, 16))),
    }


def rounded_sum(partial_value):
    kept = lax.optimization_barrier(partial_value.astype(jnp.bfloat16))
    return jnp.sum(kept.astype(jnp.float32), axis=1)


def expert_pass(rows_in, scaled_grads, gate_w, up_w, down_w):
    row_total = rows_in.shape[0]
    blocks = rows_in.astype(jnp.float32).reshape(row_total, N_CTX, FEAT)
    gate_blocks = gate_w.astype(jnp.float32).reshape(N_CTX, FEAT, HID)
    up_blocks = up_w.astype(jnp.float32).reshape(N_CTX, FEAT, HID)
    gate_pre = rounded_sum(jnp.einsum('rcd,cdh->rch', blocks, gate_blocks, precision=lax.Precision.HIGHEST))
    up_proj = rounded_sum(jnp.einsum('rcd,cdh->rch', blocks, up_blocks, precision=lax.Precision.HIGHEST))
    sigmoid_gate = jax.nn.sigmoid(gate_pre)
    silu_gate = gate_pre * sigmoid_gate
    activation = (silu_gate * up_proj).astype(jnp.bfloat16)
    rows_out = jnp.dot(activation, down_w, preferred_element_type=jnp.float32).astype(jnp.bfloat16)
    grad_blocks = scaled_grads.astype(jnp.float32).reshape(row_total, N_CTX, FEAT)
    down_blocks = down_w.astype(jnp.float32).reshape(HID, N_CTX, FEAT)
    act_grad = rounded_sum(jnp.einsum('rcd,hcd->rch', grad_blocks, down_blocks, precision=lax.Precision.HIGHEST))
    gate_delta = (act_grad * up_proj * sigmoid_gate * (1.0 + gate_pre * (1.0 - sigmoid_gate))).astype(jnp.bfloat16)
    up_delta = (act_grad * silu_gate).astype(jnp.bfloat16)
    grads_out = (jnp.dot(gate_delta, gate_w.T, preferred_element_type=jnp.float32)
                 + jnp.dot(up_delta, up_w.T, preferred_element_type=jnp.float32)).astype(jnp.bfloat16)
    gate_grad = jnp.dot(rows_in.T, gate_delta, preferred_element_type=jnp.float32).astype(jnp.bfloat16)
    up_grad = jnp.dot(rows_in.T, up_delta, preferred_element_type=jnp.float32).astype(jnp.bfloat16)
    down_grad = jnp.dot(activation.T, scaled_grads, preferred_element_type=jnp.float32).astype(jnp.bfloat16)
    return rows_out, grads_out, gate_grad, up_grad, down_grad


def reference(tokens, expert_ids, route_weights, output_grad, w_gate, w_up, w_down):
    block_total = TOKENS // TOK_E
    row_total = block_total * CAP
    blank_row = jnp.zeros((1, D), jnp.bfloat16)
    padded = jnp.concatenate([tokens, blank_row], axis=0)
    padded_grad = jnp.concatenate([output_grad, blank_row], axis=0)
    token_index = jnp.arange(TOKENS, dtype=jnp.int32)
    block_of = (token_index // TOK_E).astype(jnp.int32)

    def per_expert(totals, weights_now):
        mixed_acc, grad_acc, weight_acc = totals
        gate_w, up_w, down_w, expert = weights_now
        matches = expert_ids == expert
        member = jnp.any(matches, axis=1)
        weight_tok = jnp.sum(jnp.where(matches, route_weights, 0.0), axis=1)
        marked = member.astype(jnp.int32).reshape(block_total, TOK_E)
        ranking = (jnp.cumsum(marked, axis=1) - marked).astype(jnp.int32).reshape(-1)
        where_row = jnp.where(member, block_of * CAP + ranking, row_total).astype(jnp.int32)
        slot_token = jnp.full((row_total,), TOKENS, jnp.int32).at[where_row].set(token_index, mode='drop')
        rows_in = padded[slot_token]
        grads_in = padded_grad[slot_token]
        slot_weight = jnp.concatenate([weight_tok, jnp.zeros((1,), jnp.float32)])[slot_token]
        scaled_grads = (grads_in.astype(jnp.float32) * slot_weight[:, None]).astype(jnp.bfloat16)
        rows_out, grads_out, gate_grad, up_grad, down_grad = expert_pass(rows_in, scaled_grads, gate_w, up_w, down_w)
        mixed_acc = mixed_acc.at[slot_token].add(slot_weight[:, None] * rows_out.astype(jnp.float32), mode='drop')
        grad_acc = grad_acc.at[slot_token].add(grads_out.astype(jnp.float32), mode='drop')
        products = jnp.sum(grads_in.astype(jnp.float32) * rows_out.astype(jnp.float32), axis=1)
        token_dots = jnp.zeros((TOKENS,), jnp.float32).at[slot_token].add(products, mode='drop')
        weight_acc = weight_acc + jnp.where(matches, token_dots[:, None], 0.0)
        return (mixed_acc, grad_acc, weight_acc), (gate_grad, up_grad, down_grad)

    start_totals = (jnp.zeros((TOKENS, D), jnp.float32), jnp.zeros((TOKENS, D), jnp.float32),
                    jnp.zeros((TOKENS, TOP), jnp.float32))
    expert_list = jnp.arange(EXPERTS, dtype=jnp.int32)
    final, stacked = lax.scan(per_expert, start_totals, (w_gate, w_up, w_down, expert_list))
    mixed_acc, grad_acc, weight_acc = final
    gate_grad, up_grad, down_grad = stacked
    return (mixed_acc.astype(jnp.bfloat16), grad_acc.astype(jnp.bfloat16), weight_acc,
            gate_grad, up_grad, down_grad)
```

```python
import functools

import jax
import jax.numpy as jnp
from jax import lax
from jax.experimental import pallas as pl
from jax.experimental.pallas import tpu as pltpu
from jax.sharding import PartitionSpec as P

F32 = jnp.float32
BF16 = jnp.bfloat16
TILE = 256
LANE = 128
FEAT = 448
HID = 2048
TOKS = 1024
BOTH = ("ctx", "exp")
VM = pl.BlockSpec(memory_space=pltpu.VMEM)
SM = pl.BlockSpec(memory_space=pltpu.SMEM)
ANY = pl.BlockSpec(memory_space=pl.ANY)


def params(mib):
    return pltpu.CompilerParams(vmem_limit_bytes=mib * 1024 * 1024)


def cost(flops, nbytes):
    return pl.CostEstimate(flops=int(flops), bytes_accessed=int(nbytes), transcendentals=0)


def sds(shape, dtype):
    return jax.ShapeDtypeStruct(shape, dtype)


def dot(a, b):
    return lax.dot_general(a, b, (((1,), (0,)), ((), ())), preferred_element_type=F32)


def dot_t(a, b):
    return lax.dot_general(a, b, (((1,), (1,)), ((), ())), preferred_element_type=F32)


def hop(v, axis):
    pairs = []
    for y in range(4):
        for x in range(4):
            for e in range(8):
                s = 1 if e % 2 == 0 else -1
                to = (y * 4 + (x + s) % 4) if axis == "x" else (((y + s) % 4) * 4 + x)
                pairs.append(((y * 4 + x) * 8 + e, to * 8 + e))
    return lax.ppermute(v, BOTH, pairs)


def z_shift(v, k):
    return lax.ppermute(v, "exp", [(z * 2 + c, ((z + k) % 4) * 2 + c) for z in range(4) for c in range(2)])


def mate(v):
    return lax.ppermute(v, "exp", [(e, e ^ 1) for e in range(8)])


def place(info):
    ctx = info[0]
    y = ctx // 4
    x = ctx - y * 4
    core = info[1] - (info[1] // 2) * 2
    return x, y, 1 - 2 * core


def mod4(v):
    return jnp.bitwise_and(v + 8, 3)


def scatter_col(info, stream, outer, inner):
    x, y, s = place(info)
    jx, jy = (outer, inner) if stream == 0 else (inner, outer)
    return mod4(y + s * (3 - jy)) * 4 + mod4(x + s * (3 - jx))


def gather_col(info, stream, outer, inner):
    x, y, s = place(info)
    kx, ky = (inner, outer) if stream == 0 else (outer, inner)
    return mod4(y - s * ky) * 4 + mod4(x - s * kx)


def lanes(c):
    return pl.ds(pl.multiple_of(c * LANE, LANE), LANE)


def pack_kernel(tok, ids, rw, out):
    out[:FEAT, :] = tok[...]
    expert = lax.broadcasted_iota(jnp.int32, (16, LANE), 0)
    dense = jnp.zeros((16, LANE), F32)
    for k in range(8):
        dense += jnp.where(ids[k : k + 1, :] == expert, rw[k : k + 1, :], 0.0)
    for i, part in enumerate(split3(dense)):
        out[FEAT + 16 * i : FEAT + 16 * (i + 1), :] = part


def split3(v):
    hi = v.astype(BF16)
    rest = v - hi.astype(F32)
    mid = rest.astype(BF16)
    low = (rest - mid.astype(F32)).astype(BF16)
    return hi, mid, low


def pack(tok, ids, rw):
    return pl.pallas_call(pack_kernel, out_shape=sds((FEAT + 48, LANE), BF16), in_specs=[VM] * 3, out_specs=VM)(
        tok, ids, rw
    )


def rows_kernel(nt, info, mine, other, xr, xt, pt, wcol, wrow, meta):
    blocks = [mine[j] for j in range(4)] + [other[j] for j in range(4)]
    tt = jnp.concatenate([b[:FEAT, :] for b in blocks], axis=1)
    expert = lax.broadcasted_iota(jnp.int32, (16, LANE), 0)
    first = info[1] * 2
    weights = [[], []]
    for b in blocks:
        tail = b[FEAT : FEAT + 48, :].astype(F32)
        dense = (tail[:16] + tail[16:32]) + tail[32:48]
        for l in range(2):
            weights[l].append(jnp.sum(jnp.where(expert == first + l, dense, 0.0), axis=0, keepdims=True))
    member = [[(w > 0.0).astype(F32) for w in ws] for ws in weights]
    before = (
        lax.broadcasted_iota(jnp.int32, (LANE, LANE), 0) < lax.broadcasted_iota(jnp.int32, (LANE, LANE), 1)
    ).astype(BF16)
    ranks = dot(jnp.concatenate(member[0] + member[1], axis=0).astype(BF16), before)
    slots = []
    base = jnp.zeros((1, 1), F32)
    for l in range(2):
        run = base
        for b in range(8):
            m = member[l][b]
            slots.append(jnp.where(m > 0.0, ranks[l * 8 + b : l * 8 + b + 1, :] + run, -1.0))
            run = run + jnp.sum(m, axis=1, keepdims=True)
        if l == 0:
            base = jnp.maximum(jnp.floor((run + (TILE - 1.0)) * (1.0 / TILE)), 1.0) * TILE
    count = jnp.sum(jnp.concatenate(member[0], axis=0)).astype(jnp.int32)
    meta[0] = jnp.maximum((count + (TILE - 1)) // TILE, 1)
    count = jnp.sum(jnp.concatenate(member[1], axis=0)).astype(jnp.int32)
    meta[1] = jnp.maximum((count + (TILE - 1)) // TILE, 1)
    q0 = jnp.concatenate(slots[:8], axis=1).astype(jnp.int32)
    q1 = jnp.concatenate(slots[8:], axis=1).astype(jnp.int32)
    w0 = jnp.concatenate(weights[0], axis=1)
    w1 = jnp.concatenate(weights[1], axis=1)
    for i in range(nt):
        sl = slice(i * TILE, (i + 1) * TILE)
        row = lax.broadcasted_iota(jnp.int32, (TILE, TOKS), 0) + i * TILE
        hit0, hit1 = row == q0, row == q1
        one = jnp.where(hit0 | hit1, 1.0, 0.0).astype(BF16)
        pt[sl, :] = one
        col = jnp.sum(jnp.where(hit0, w0, 0.0) + jnp.where(hit1, w1, 0.0), axis=1, keepdims=True)
        wide = jnp.broadcast_to(col, (TILE, LANE))
        wcol[sl, :] = wide
        wrow[:, sl] = jnp.transpose(wide)[:8, :]
        xr[sl, :] = dot_t(one, tt).astype(BF16)
        xt[:, sl] = dot_t(tt, one).astype(BF16)


def make_rows(nt, info, mine, other):
    r = nt * TILE
    return pl.pallas_call(
        functools.partial(rows_kernel, nt),
        out_shape=(
            sds((r, FEAT), BF16),
            sds((FEAT, r), BF16),
            sds((r, TOKS), BF16),
            sds((r, LANE), F32),
            sds((8, r), F32),
            sds((8,), jnp.int32),
        ),
        in_specs=[SM, VM, VM],
        out_specs=(VM, VM, VM, VM, VM, SM),
        compiler_params=params(40),
        cost_estimate=cost(4 * r * TOKS * FEAT, 8e6),
    )(info, mine, other)


def grads_kernel(nt, mine, other, pt, wcol, wrow, gr, gt):
    gg = jnp.concatenate([mine[j] for j in range(4)] + [other[j] for j in range(4)], axis=1)
    for i in range(nt):
        sl = slice(i * TILE, (i + 1) * TILE)
        one = pt[sl, :]
        gr[sl, :] = (dot_t(one, gg) * wcol[sl, :1]).astype(BF16)
        gt[:, sl] = (dot_t(gg, one) * wrow[:1, sl]).astype(BF16)


def make_grads(nt, mine, other, pt, wcol, wrow):
    r = nt * TILE
    return pl.pallas_call(
        functools.partial(grads_kernel, nt),
        out_shape=(sds((r, FEAT), BF16), sds((FEAT, r), BF16)),
        in_specs=[VM] * 5,
        out_specs=(VM, VM),
        compiler_params=params(40),
        cost_estimate=cost(4 * r * TOKS * FEAT, 8e6),
    )(mine, other, pt, wcol, wrow)


def parts_kernel(step, pieces, n_w, info, meta, src, *refs):
    weights, refs = refs[:n_w], refs[n_w:]
    outs, refs = refs[: len(pieces)], refs[len(pieces) :]
    bufs, sems = refs[: len(pieces)], refs[len(pieces)]
    copies = []
    for n, (stream, w, lo, rows) in enumerate(pieces):
        for i in range(4):
            c = scatter_col(info, stream, step, i)
            copies.append(
                pltpu.make_async_copy(
                    weights[w].at[:, :, lanes(c)], bufs[n].at[:, :, pl.ds(i * LANE, LANE)], sems.at[n * 4 + i]
                )
            )
    for cp in copies:
        cp.start()
    tiles0 = meta[0]
    for n, (stream, w, lo, rows) in enumerate(pieces):
        for i in range(4):
            copies[n * 4 + i].wait()
        at = lo
        while at < lo + rows:
            end = min((at // TILE + 1) * TILE, lo + rows)
            e = (at // TILE >= tiles0).astype(jnp.int32)
            out = dot(src[at:end, :], bufs[n][e]).astype(BF16)
            for i in range(4):
                outs[n][i, at - lo : end - lo, :] = out[:, i * LANE : (i + 1) * LANE]
            at = end


def parts(step, pieces, info, meta, src, weights):
    total = sum(p[3] for p in pieces)
    return pl.pallas_call(
        functools.partial(parts_kernel, step, pieces, len(weights)),
        out_shape=tuple(sds((4, p[3], LANE), BF16) for p in pieces),
        in_specs=[SM, SM, VM] + [ANY] * len(weights),
        out_specs=tuple(VM for _ in pieces),
        scratch_shapes=[pltpu.VMEM((2, FEAT, 512), BF16) for _ in pieces]
        + [pltpu.SemaphoreType.DMA((4 * len(pieces),))],
        compiler_params=params(24),
        cost_estimate=cost(2 * total * FEAT * 512, 6e6),
    )(info, meta, src, *weights)


def delta_kernel(r, go, gi, uo, ui, aoa, aia, aob, aib, wcol, gd, ud):
    half = r // 2
    zero = jnp.zeros((16, LANE), BF16)
    gd[r:, :] = zero
    ud[r:, :] = zero
    hi_rows, lo_rows = [], []
    for i in range(r // LANE):
        sl = slice(i * LANE, (i + 1) * LANE)
        gate = go[sl, :].astype(F32) + gi[sl, :].astype(F32)
        up = uo[sl, :].astype(F32) + ui[sl, :].astype(F32)
        if (i + 1) * LANE <= half:
            ag = aoa[sl, :].astype(F32) + aia[sl, :].astype(F32)
        else:
            sh = slice(i * LANE - half, (i + 1) * LANE - half)
            ag = aob[sh, :].astype(F32) + aib[sh, :].astype(F32)
        s = 1.0 / (1.0 + jnp.exp(-gate))
        silu = gate * s
        gd[sl, :] = (ag * up * s * (1.0 + gate * (1.0 - s))).astype(BF16)
        ud[sl, :] = (ag * silu).astype(BF16)
        act = (silu * up).astype(BF16).astype(F32)
        w = wcol[sl, :]
        inner = act * ag * jnp.where(w > 0.0, 1.0 / jnp.maximum(w, 1e-6), 0.0)
        total = jnp.sum(jnp.transpose(inner), axis=0, keepdims=True)
        hi = total.astype(BF16)
        hi_rows.append(hi)
        lo_rows.append((total - hi.astype(F32)).astype(BF16))
    fill = [jnp.zeros((1, LANE), BF16)] * (16 - len(hi_rows))
    gd[r:, :] = jnp.concatenate(hi_rows + fill, axis=0)
    ud[r:, :] = jnp.concatenate(lo_rows + fill, axis=0)


def make_deltas(r, *args):
    return pl.pallas_call(
        functools.partial(delta_kernel, r),
        out_shape=(sds((r + 16, LANE), BF16), sds((r + 16, LANE), BF16)),
        in_specs=[VM] * 9,
        out_specs=(VM, VM),
        compiler_params=params(24),
        cost_estimate=cost(r * LANE * 40, 3e6),
    )(*args)


def down_kernel(nt, info, meta, w, gt, wrow, pt, *refs):
    bufs, (mixed, dgrad), (act, mix, sems) = refs[:8], refs[8:10], refs[10:]
    half = nt * TILE // 2
    copies = []
    for stream in range(2):
        for k in range(4):
            for j in range(4):
                c = gather_col(info, stream, k, j)
                copies.append(
                    pltpu.make_async_copy(
                        bufs[stream * 4 + k].at[j],
                        act.at[pl.ds(stream * half, half), lanes(c)],
                        sems.at[stream * 16 + k * 4 + j],
                    )
                )
    for cp in copies:
        cp.start()
    for cp in copies:
        cp.wait()
    tiles0, tiles1 = meta[0], meta[1]
    mix[...] = jnp.zeros_like(mix)

    def tile_step(i, carry):
        rows = pl.ds(pl.multiple_of(i * TILE, TILE), TILE)
        e = (i >= tiles0).astype(jnp.int32)
        out = dot_t(w[e], act[rows, :])
        out = (out * wrow[:1, rows]).astype(BF16)
        mix[...] += dot(out, pt[rows, :])
        return carry

    lax.fori_loop(0, tiles0 + tiles1, tile_step, 0)
    for b in range(8):
        mixed[b] = mix[:, b * LANE : (b + 1) * LANE].astype(BF16)
    for e in range(2):
        lo = tiles0 * e
        hi = tiles0 + tiles1 * e

        def chunk(n, carry, lo=lo, hi=hi, e=e):
            cols = pl.ds(pl.multiple_of(n * 512, 512), 512)

            def add(i, acc):
                rows = pl.ds(pl.multiple_of(i * TILE, TILE), TILE)
                return acc + dot(gt[:, rows], act[rows, cols])

            acc = lax.fori_loop(lo, hi, add, jnp.zeros((FEAT, 512), F32))
            dgrad[e, :, cols] = acc.astype(BF16)
            return carry

        lax.fori_loop(0, HID // 512, chunk, 0)


def down(nt, info, meta, w, gt, wrow, pt, bufs):
    r = nt * TILE
    return pl.pallas_call(
        functools.partial(down_kernel, nt),
        out_shape=(sds((8, FEAT, LANE), BF16), sds((2, FEAT, HID), BF16)),
        in_specs=[SM, SM, VM, VM, VM, VM] + [ANY] * 8,
        out_specs=(VM, VM),
        scratch_shapes=[
            pltpu.VMEM((r, HID), BF16),
            pltpu.VMEM((FEAT, TOKS), F32),
            pltpu.SemaphoreType.DMA((32,)),
        ],
        compiler_params=params(48),
        cost_estimate=cost(4 * r * FEAT * HID + 2 * r * FEAT * TOKS, 2e7),
    )(info, meta, w, gt, wrow, pt, *bufs)


def wgrad_kernel(nt, ks, fresh, info, meta, xt, *refs):
    n = len(ks)
    bufs = (refs[:n], refs[n : 2 * n])
    refs = refs[2 * n :] if fresh else refs[2 * n + 2 :]
    outs, (land, stage, in_sems, out_sems) = refs[:2], refs[2:]
    r = nt * TILE
    tiles0, tiles1 = meta[0], meta[1]
    work = [(a, m) for m in range(n) for a in range(2)]

    def fetch(t):
        a, m = work[t]
        return [
            pltpu.make_async_copy(
                bufs[a][m].at[j, pl.ds(0, r), :], land.at[t % 2, :, pl.ds(j * LANE, LANE)], in_sems.at[t % 2, j]
            )
            for j in range(4)
        ]

    def store(t):
        a, m = work[t]
        return [
            pltpu.make_async_copy(
                stage.at[t % 2, :, :, pl.ds(j * LANE, LANE)],
                outs[a].at[:, :, lanes(gather_col(info, a, ks[m], j))],
                out_sems.at[t % 2, j],
            )
            for j in range(4)
        ]

    for cp in fetch(0):
        cp.start()
    for t in range(len(work)):
        if t + 1 < len(work):
            for cp in fetch(t + 1):
                cp.start()
        for cp in fetch(t):
            cp.wait()
        if t >= 2:
            for cp in store(t - 2):
                cp.wait()
        for e in range(2):

            def add(i, acc, t=t):
                rows = pl.ds(pl.multiple_of(i * TILE, TILE), TILE)
                return acc + dot(xt[:, rows], land[t % 2, rows, :])

            acc = lax.fori_loop(tiles0 * e, tiles0 + tiles1 * e, add, jnp.zeros((FEAT, 512), F32))
            stage[t % 2, e] = acc.astype(BF16)
        for cp in store(t):
            cp.start()
    for t in range(max(0, len(work) - 2), len(work)):
        for cp in store(t):
            cp.wait()


def wgrad(nt, ks, info, meta, xt, gds, uds, prev):
    r = nt * TILE
    n = len(ks)
    shape = sds((2, FEAT, HID), BF16)
    args = [info, meta, xt, *gds, *uds]
    alias = {}
    if prev is not None:
        alias = {len(args): 0, len(args) + 1: 1}
        args += list(prev)
    return pl.pallas_call(
        functools.partial(wgrad_kernel, nt, ks, prev is None),
        out_shape=(shape, shape),
        in_specs=[SM, SM, VM] + [ANY] * (len(args) - 3),
        out_specs=(ANY, ANY),
        scratch_shapes=[
            pltpu.VMEM((2, r, 512), BF16),
            pltpu.VMEM((2, 2, FEAT, 512), BF16),
            pltpu.SemaphoreType.DMA((2, 4)),
            pltpu.SemaphoreType.DMA((2, 4)),
        ],
        input_output_aliases=alias,
        compiler_params=params(32),
        cost_estimate=cost(4 * n * r * FEAT * 512, 1e7),
    )(*args)


def back_kernel(nt, ks, first, last, info, meta, *refs):
    n = len(ks)
    r = nt * TILE
    refs = list(refs)
    prev = None if first else (refs.pop(0), refs.pop(0))
    pt = refs.pop(0) if last else None
    bufs = (refs[:n], refs[n : 2 * n])
    ws = refs[2 * n : 2 * n + 2]
    refs = refs[2 * n + 2 :]
    if last:
        (out,), (acc, inner, land, wl, in_sems, s_land, s_sems) = refs[:1], refs[1:]
    else:
        (acc, inner), (land, wl, in_sems, s_land, s_sems) = refs[:2], refs[2:]
    tiles0, tiles1 = meta[0], meta[1]
    work = [(a, m) for m in range(n) for a in range(2)]

    def fetch(t):
        a, m = work[t]
        cps = []
        for j in range(4):
            cps.append(
                pltpu.make_async_copy(
                    bufs[a][m].at[j, pl.ds(0, r), :], land.at[t % 2, :, pl.ds(j * LANE, LANE)], in_sems.at[t % 2, j]
                )
            )
            c = gather_col(info, a, ks[m], j)
            cps.append(
                pltpu.make_async_copy(
                    ws[a].at[:, :, lanes(c)], wl.at[t % 2, :, :, pl.ds(j * LANE, LANE)], in_sems.at[t % 2, 4 + j]
                )
            )
        return cps

    sums = [
        pltpu.make_async_copy(bufs[a][m].at[:, pl.ds(r, 16), :], s_land.at[t], s_sems.at[t])
        for t, (a, m) in enumerate(work)
    ]
    for cp in fetch(0):
        cp.start()
    for cp in sums:
        cp.start()
    if first:
        acc[...] = jnp.zeros_like(acc)
        inner[...] = jnp.zeros_like(inner)
    else:
        acc[...] = prev[0][...]
        inner[...] = prev[1][...]
    for t in range(len(work)):
        if t + 1 < len(work):
            for cp in fetch(t + 1):
                cp.start()
        for cp in fetch(t):
            cp.wait()

        def step(i, carry, t=t):
            rows = pl.ds(pl.multiple_of(i * TILE, TILE), TILE)
            e = (i >= tiles0).astype(jnp.int32)
            acc[:, rows] += dot_t(wl[t % 2, e], land[t % 2, rows, :])
            return carry

        lax.fori_loop(0, tiles0 + tiles1, step, 0)
    for t in range(len(work)):
        sums[t].wait()
        for j in range(4):
            inner[...] += s_land[t, j].astype(F32)
    if last:
        total = jnp.zeros((FEAT, TOKS), F32)
        dense = [jnp.zeros((1, TOKS), F32), jnp.zeros((1, TOKS), F32)]
        s_all = inner[...]
        s3 = split3(s_all)
        for i in range(nt):
            sl = slice(i * TILE, (i + 1) * TILE)
            total = total + dot(acc[:, sl].astype(BF16), pt[sl, :])
            row = jnp.zeros((1, TOKS), F32)
            for c in range(2 * i, 2 * i + 2):
                got = dot(
                    jnp.concatenate([p[c : c + 1, :] for p in s3] + [jnp.zeros((5, LANE), BF16)], axis=0),
                    pt[c * LANE : (c + 1) * LANE, :],
                )
                row += (got[0:1] + got[1:2]) + got[2:3]
            is1 = (i >= tiles0).astype(F32)
            dense[0] += row * (1.0 - is1)
            dense[1] += row * is1
        expert = lax.broadcasted_iota(jnp.int32, (16, TOKS), 0)
        at = info[1] * 2
        table = jnp.where(expert == at, dense[0], 0.0) + jnp.where(expert == at + 1, dense[1], 0.0)
        t3 = split3(table)
        for b in range(8):
            cols = slice(b * LANE, (b + 1) * LANE)
            out[b, :FEAT, :] = total[:, cols].astype(BF16)
            for q in range(3):
                out[b, FEAT + 16 * q : FEAT + 16 * (q + 1), :] = t3[q][:, cols]


def back(nt, ks, info, meta, gds, uds, wg, wu, prev, pt):
    r = nt * TILE
    n = len(ks)
    first, last = prev is None, pt is not None
    args = [info, meta]
    specs = [SM, SM]
    if not first:
        args += list(prev)
        specs += [VM, VM]
    if last:
        args.append(pt)
        specs.append(VM)
    args += [*gds, *uds, wg, wu]
    specs += [ANY] * (2 * n + 2)
    keep = [((FEAT, r), F32), ((16, LANE), F32)]
    scratch = [
        pltpu.VMEM((2, r, 512), BF16),
        pltpu.VMEM((2, 2, FEAT, 512), BF16),
        pltpu.SemaphoreType.DMA((2, 8)),
        pltpu.VMEM((2 * n, 4, 16, LANE), BF16),
        pltpu.SemaphoreType.DMA((2 * n,)),
    ]
    if last:
        out_shape = sds((8, FEAT + 48, LANE), BF16)
        out_specs = VM
        scratch = [pltpu.VMEM(*k) for k in keep] + scratch
    else:
        out_shape = tuple(sds(*k) for k in keep)
        out_specs = (VM, VM)
    return pl.pallas_call(
        functools.partial(back_kernel, nt, ks, first, last),
        out_shape=out_shape,
        in_specs=specs,
        out_specs=out_specs,
        scratch_shapes=scratch,
        compiler_params=params(40),
        cost_estimate=cost(4 * n * r * FEAT * 512, 1e7),
    )(*args)


def home_kernel(own, other, ids, tg, wg):
    total = own[...].astype(F32)
    for j in range(3):
        total = total + other[j][...].astype(F32)
    tg[...] = total[:FEAT].astype(BF16)
    dense = (total[FEAT : FEAT + 16] + total[FEAT + 16 : FEAT + 32]) + total[FEAT + 32 :]
    expert = lax.broadcasted_iota(jnp.int32, (16, LANE), 0)
    for k in range(8):
        wg[k : k + 1, :] = jnp.sum(jnp.where(expert == ids[k : k + 1, :], dense, 0.0), axis=0, keepdims=True)


def home(own, a, b, c, ids):
    def kern(own, a, b, c, ids, tg, wg):
        home_kernel(own, (a, b, c), ids, tg, wg)

    return pl.pallas_call(
        kern,
        out_shape=(sds((FEAT, LANE), BF16), sds((8, LANE), F32)),
        in_specs=[VM] * 5,
        out_specs=(VM, VM),
    )(own, a, b, c, ids)


def to_experts(v):
    got = [v] + [z_shift(v, -k) for k in (1, 2, 3)]
    mine = jnp.stack(got)
    return mine, mate(mine)


def to_home(v):
    there = mate(v[4:])
    mine = (v[:4].astype(F32) + there.astype(F32)).astype(BF16)
    return [mine[0]] + [z_shift(mine[k], k) for k in (1, 2, 3)]


def add(a, b):
    return (a.astype(F32) + b.astype(F32)).astype(BF16)


def ring_sum(pieces, axes):
    cur = pieces[0]
    for j in (1, 2):
        cur = add(hop(cur, axes[0]), pieces[j])
    got = hop(cur, axes[0])
    cur = add(got[0], pieces[3][0])
    for i in (1, 2):
        near = hop(cur, axes[1])
        cur = (near.astype(F32) + (got[i].astype(F32) + pieces[3][i].astype(F32))).astype(BF16)
    return hop(cur, axes[1]), add(got[3], pieces[3][3])


def ring_gather(v, axes):
    line = [v]
    for _ in range(3):
        line.append(hop(line[-1], axes[0]))
    out = [jnp.stack(line)]
    for _ in range(3):
        out.append(hop(out[-1], axes[1]))
    return out


def passes(nt, info, mine, other, og_mine, og_other, w_gate, w_up, w_down):
    r = nt * TILE
    half = r // 2
    xy, yx = ("x", "y"), ("y", "x")
    xr, xt, pt, wcol, wrow, meta = make_rows(nt, info, mine, other)
    gate_up = [parts(j, ((0, 0, 0, r), (1, 1, 0, r)), info, meta, xr, (w_gate, w_up)) for j in range(4)]
    gr, gt = make_grads(nt, og_mine, og_other, pt, wcol, wrow)
    act_parts = [parts(j, ((0, 0, 0, half), (1, 0, half, half)), info, meta, gr, (w_down,)) for j in range(4)]
    gate_in, gate_own = ring_sum([p[0] for p in gate_up], xy)
    up_in, up_own = ring_sum([p[1] for p in gate_up], yx)
    a_in, a_own = ring_sum([p[0] for p in act_parts], xy)
    b_in, b_own = ring_sum([p[1] for p in act_parts], yx)
    gate_pre = gate_in.astype(F32) + gate_own.astype(F32)
    act = (gate_pre * jax.nn.sigmoid(gate_pre) * (up_in.astype(F32) + up_own.astype(F32))).astype(BF16)
    act_bufs = ring_gather(act[:half], xy) + ring_gather(act[half:], yx)
    gd, ud = make_deltas(r, gate_own, gate_in, up_own, up_in, a_own, a_in, b_own, b_in, wcol)
    gd_bufs = ring_gather(gd, xy)
    ud_bufs = ring_gather(ud, yx)
    mixed_parts, down_grad = down(nt, info, meta, w_down, gt, wrow, pt, act_bufs)
    early = (0, 1, 2)
    acc = back(nt, early, info, meta, gd_bufs[:3], ud_bufs[:3], w_gate, w_up, None, None)
    grads = wgrad(nt, early, info, meta, xt, gd_bufs[:3], ud_bufs[:3], None)
    token_parts = back(nt, (3,), info, meta, gd_bufs[3:], ud_bufs[3:], w_gate, w_up, acc, pt)
    gate_grad, up_grad = wgrad(nt, (3,), info, meta, xt, gd_bufs[3:], ud_bufs[3:], grads)
    mixed_home = to_home(mixed_parts)
    mixed = sum(m.astype(F32) for m in mixed_home).astype(BF16)
    return mixed, tuple(to_home(token_parts)), gate_grad, up_grad, down_grad


def body(tokens, expert_ids, route_weights, output_grad, w_gate, w_up, w_down):
    info = jnp.stack([lax.axis_index("ctx"), lax.axis_index("exp")]).astype(jnp.int32)
    ids = expert_ids.T
    mine, other = to_experts(pack(tokens.T, ids, route_weights.T))
    og_mine, og_other = to_experts(output_grad.T)
    mixed, token_home, gate_grad, up_grad, down_grad = passes(
        6, info, mine, other, og_mine, og_other, w_gate, w_up, w_down.transpose(0, 2, 1)
    )
    token_grad, weight_grad = home(*token_home, ids)
    return (
        mixed.T,
        token_grad.T,
        weight_grad.T,
        gate_grad,
        up_grad,
        down_grad.transpose(0, 2, 1),
    )


def solution(mesh):
    return jax.shard_map(
        body,
        mesh=mesh,
        in_specs=(
            P("exp", "ctx"),
            P("exp", None),
            P("exp", None),
            P("exp", "ctx"),
            P("exp", "ctx", None),
            P("exp", "ctx", None),
            P("exp", None, "ctx"),
        ),
        out_specs=(
            P("exp", "ctx"),
            P("exp", "ctx"),
            P("exp", None),
            P("exp", "ctx", None),
            P("exp", "ctx", None),
            P("exp", None, "ctx"),
        ),
        check_vma=False,
    )
```

```python
import functools

import jax
import jax.numpy as jnp
from jax import lax
from jax.experimental import pallas as pl
from jax.experimental.pallas import tpu as pltpu
from jax.sharding import PartitionSpec as P

F32 = jnp.float32
BF16 = jnp.bfloat16
TILE = 256
LANE = 128
FEAT = 448
HID = 2048
SPAN = 768
PAD = 2 * SPAN
LEAVE = (2, 1, -1, 0)
ARRIVE = (0, 1, -1, 2)
TOKS = 1024
BOTH = ("ctx", "exp")
VM = pl.BlockSpec(memory_space=pltpu.VMEM)
SM = pl.BlockSpec(memory_space=pltpu.SMEM)
ANY = pl.BlockSpec(memory_space=pl.ANY)


def params(mib):
    return pltpu.CompilerParams(vmem_limit_bytes=mib * 1024 * 1024)


def sds(shape, dtype):
    return jax.ShapeDtypeStruct(shape, dtype)


def call(kern, args, specs, out_shape, out_specs, scratch=(), after=(), mib=32, alias=None):
    n_in, n_out = len(args), len(out_shape)
    skip = n_in + len(after)

    def wrapped(*refs):
        kern(*refs[:n_in], *refs[skip : skip + n_out], *refs[skip + n_out + 1 :])

    res = pl.pallas_call(
        wrapped,
        out_shape=(*out_shape, sds((8, LANE), F32)),
        in_specs=[*specs] + [ANY] * len(after),
        out_specs=(*out_specs, ANY),
        scratch_shapes=list(scratch),
        input_output_aliases=alias or {},
        compiler_params=params(mib),
        cost_estimate=pl.CostEstimate(flops=1, bytes_accessed=1, transcendentals=0),
    )(*args, *after)
    return res[:-1], res[-1]


def dot(a, b):
    return lax.dot_general(a, b, (((1,), (0,)), ((), ())), preferred_element_type=F32)


def dot_t(a, b):
    return lax.dot_general(a, b, (((1,), (1,)), ((), ())), preferred_element_type=F32)


def hop(v, phase, step):
    pairs = []
    for y in range(4):
        for x in range(4):
            for e in range(8):
                along_x = (e % 2 == 0) == (phase == 0)
                to = (y * 4 + (x + step) % 4) if along_x else (((y + step) % 4) * 4 + x)
                pairs.append(((y * 4 + x) * 8 + e, to * 8 + e))
    return lax.ppermute(v, BOTH, pairs)


def z_shift(v, k):
    return lax.ppermute(v, "exp", [(z * 2 + c, ((z + k) % 4) * 2 + c) for z in range(4) for c in range(2)])


def mate(v):
    return lax.ppermute(v, "exp", [(e, e ^ 1) for e in range(8)])


def block_at(info, d0, d1):
    ctx = info[0]
    y = ctx // 4
    x = ctx - y * 4
    odd = info[1] - (info[1] // 2) * 2
    dx = d0 + odd * (d1 - d0)
    dy = d1 + odd * (d0 - d1)
    return jnp.bitwise_and(y + dy + 8, 3) * 4 + jnp.bitwise_and(x + dx + 8, 3)


def lanes(c):
    return pl.ds(pl.multiple_of(c * LANE, LANE), LANE)


def pack_kernel(tok, ids, rw, out):
    out[:FEAT, :] = tok[...]
    expert = lax.broadcasted_iota(jnp.int32, (16, LANE), 0)
    dense = jnp.zeros((16, LANE), F32)
    for k in range(8):
        dense += jnp.where(ids[k : k + 1, :] == expert, rw[k : k + 1, :], 0.0)
    for i, part in enumerate(split3(dense)):
        out[FEAT + 16 * i : FEAT + 16 * (i + 1), :] = part


def split3(v):
    hi = v.astype(BF16)
    rest = v - hi.astype(F32)
    mid = rest.astype(BF16)
    low = (rest - mid.astype(F32)).astype(BF16)
    return hi, mid, low


def pack(tok, ids, rw):
    return pl.pallas_call(pack_kernel, out_shape=sds((FEAT + 48, LANE), BF16), in_specs=[VM] * 3, out_specs=VM)(
        tok, ids, rw
    )


def rows_kernel(nt, info, mine, other, xr, pt, wcol, wrow, meta, tt_out):
    blocks = [mine[j] for j in range(4)] + [other[j] for j in range(4)]
    tt = jnp.concatenate([b[:FEAT, :] for b in blocks], axis=1)
    expert = lax.broadcasted_iota(jnp.int32, (16, LANE), 0)
    first = info[1] * 2
    weights = [[], []]
    named = jnp.zeros((16, 1), F32)
    for b in blocks:
        tail = b[FEAT : FEAT + 48, :].astype(F32)
        dense = (tail[:16] + tail[16:32]) + tail[32:48]
        named += jnp.sum((dense > 0.0).astype(F32), axis=1, keepdims=True)
        for l in range(2):
            weights[l].append(jnp.sum(jnp.where(expert == first + l, dense, 0.0), axis=0, keepdims=True))
    member = [[(w > 0.0).astype(F32) for w in ws] for ws in weights]
    before = (
        lax.broadcasted_iota(jnp.int32, (LANE, LANE), 0) < lax.broadcasted_iota(jnp.int32, (LANE, LANE), 1)
    ).astype(BF16)
    ranks = dot(jnp.concatenate(member[0] + member[1], axis=0).astype(BF16), before)
    slots = []
    base = jnp.zeros((1, 1), F32)
    for l in range(2):
        run = base
        for b in range(8):
            m = member[l][b]
            slots.append(jnp.where(m > 0.0, ranks[l * 8 + b : l * 8 + b + 1, :] + run, -1.0))
            run = run + jnp.sum(m, axis=1, keepdims=True)
        if l == 0:
            base = jnp.maximum(jnp.floor((run + (TILE - 1.0)) * (1.0 / TILE)), 1.0) * TILE
    count = jnp.sum(jnp.concatenate(member[0], axis=0)).astype(jnp.int32)
    meta[0] = jnp.maximum((count + (TILE - 1)) // TILE, 1)
    count = jnp.sum(jnp.concatenate(member[1], axis=0)).astype(jnp.int32)
    meta[1] = jnp.maximum((count + (TILE - 1)) // TILE, 1)
    tiles = jnp.broadcast_to(jnp.maximum(jnp.floor((named + (TILE - 1.0)) * (1.0 / TILE)), 1.0), (16, LANE))
    even = lax.broadcasted_iota(jnp.int32, (16, 16), 0) // 2 == lax.broadcasted_iota(jnp.int32, (16, 16), 1) // 2
    most = jnp.max(dot(even.astype(BF16), tiles.astype(BF16))).astype(jnp.int32)
    meta[2] = most
    tt_out[...] = tt
    q0 = jnp.concatenate(slots[:8], axis=1).astype(jnp.int32)
    q1 = jnp.concatenate(slots[8:], axis=1).astype(jnp.int32)
    w0 = jnp.concatenate(weights[0], axis=1)
    w1 = jnp.concatenate(weights[1], axis=1)

    def tile_rows(i, carry):
        sl = pl.ds(pl.multiple_of(i * TILE, TILE), TILE)
        row = lax.broadcasted_iota(jnp.int32, (TILE, TOKS), 0) + i * TILE
        hit0, hit1 = row == q0, row == q1
        one = jnp.where(hit0 | hit1, 1.0, 0.0).astype(BF16)
        pt[sl, :] = one
        col = jnp.sum(jnp.where(hit0, w0, 0.0) + jnp.where(hit1, w1, 0.0), axis=1, keepdims=True)
        wide = jnp.broadcast_to(col, (TILE, LANE))
        wcol[sl, :] = wide
        wrow[:, sl] = jnp.transpose(wide)[:8, :]
        xr[sl, :] = dot_t(one, tt_out[...]).astype(BF16)
        return carry

    lax.fori_loop(0, nt, tile_rows, 0)


def make_rows(nt, info, mine, other, after):
    r = nt * TILE
    return call(
        functools.partial(rows_kernel, nt),
        (info, mine, other),
        [SM, VM, VM],
        (
            sds((r, FEAT), BF16),
            sds((r, TOKS), BF16),
            sds((r, LANE), F32),
            sds((8, r), F32),
            sds((8,), jnp.int32),
        ),
        (VM, VM, VM, VM, SM),
        [pltpu.VMEM((FEAT, TOKS), BF16)],
        after,
    )


def grads_kernel(nt, meta, mine, other, xr, pt, wcol, gr, xe, ge, gg, turned):
    r = nt * TILE
    off = pl.multiple_of(meta[0] * TILE, TILE)
    for j in range(4):
        gg[:, j * LANE : (j + 1) * LANE] = mine[j]
        gg[:, (j + 4) * LANE : (j + 5) * LANE] = other[j]
    if r < PAD:
        turned[:, :, r:] = jnp.zeros((2, FEAT, PAD - r), BF16)

    def tile_step(i, carry):
        sl = pl.ds(pl.multiple_of(i * TILE, TILE), TILE)
        g = (dot_t(pt[sl, :], gg[...]) * wcol[sl, :1]).astype(BF16)
        gr[sl, :] = g
        turned[0, :, sl] = jnp.transpose(xr[sl, :])
        turned[1, :, sl] = jnp.transpose(g)
        return carry

    lax.fori_loop(0, nt, tile_step, 0, unroll=nt == 5)
    mine_too = lax.broadcasted_iota(jnp.int32, (FEAT, SPAN), 1) < off
    zero = jnp.zeros((FEAT, SPAN), BF16)
    for q, out in ((0, xe), (1, ge)):
        out[0] = jnp.where(mine_too, turned[q, :, :SPAN], zero)
        out[1] = turned[q, :, pl.ds(off, SPAN)]


def make_grads(nt, meta, mine, other, xr, pt, wcol, after):
    r = nt * TILE
    span = sds((2, FEAT, SPAN), BF16)
    return call(
        functools.partial(grads_kernel, nt),
        (meta, mine, other, xr, pt, wcol),
        [SM] + [VM] * 5,
        (sds((r, FEAT), BF16), span, span),
        (VM, VM, VM),
        [pltpu.VMEM((FEAT, TOKS), BF16), pltpu.VMEM((2, FEAT, PAD), BF16)],
        after,
    )


def parts_kernel(nt, outers, split, n_w, info, meta, src, *refs):
    weights, refs = refs[:n_w], refs[n_w:]
    n_out = len(outers) * (2 if split else 1)
    outs, (bufs, sems) = refs[:n_out], refs[n_out:]
    jobs = [(p, w) for p in range(len(outers)) for w in range(n_w)]
    copies = [
        [
            pltpu.make_async_copy(
                weights[w].at[:, :, lanes(block_at(info, outers[p], LEAVE[i]))],
                bufs.at[n, :, :, pl.ds(i * LANE, LANE)],
                sems.at[n * 4 + i],
            )
            for i in range(4)
        ]
        for n, (p, w) in enumerate(jobs)
    ]
    for cps in copies:
        for cp in cps:
            cp.start()
    tiles0 = meta[0]
    for n, (p, w) in enumerate(jobs):
        for cp in copies[n]:
            cp.wait()

        def tile_step(t, carry, n=n, p=p, w=w):
            sl = pl.ds(pl.multiple_of(t * TILE, TILE), TILE)
            e = (t >= tiles0).astype(jnp.int32)
            out = dot(src[sl, :], bufs[n, e]).astype(BF16)
            for i in range(4):
                o, at = (outs[2 * p + i // 2], i % 2) if split else (outs[p], i)
                o[at, w, sl, :] = out[:, i * LANE : (i + 1) * LANE]
            return carry

        lax.fori_loop(0, nt, tile_step, 0, unroll=nt == 5)


def parts(nt, outers, split, info, meta, src, weights, after):
    n_w = len(weights)
    shape = sds((2 if split else 4, n_w, nt * TILE, LANE), BF16)
    n_out = len(outers) * (2 if split else 1)
    return call(
        functools.partial(parts_kernel, nt, outers, split, n_w),
        (info, meta, src, *weights),
        [SM, SM, VM] + [ANY] * n_w,
        (shape,) * n_out,
        (VM,) * n_out,
        [
            pltpu.VMEM((len(outers) * n_w, 2, FEAT, 512), BF16),
            pltpu.SemaphoreType.DMA((4 * len(outers) * n_w,)),
        ],
        after,
    )


def tiles_of(n, size, body):
    def step(i, carry):
        body(pl.ds(pl.multiple_of(i * size, size), size))
        return carry

    lax.fori_loop(0, n // size, step, 0)


def plus(a, b):
    return (a.astype(F32) + b.astype(F32)).astype(BF16)


def join_kernel(n_w, r, rt, lf, from_left, from_right, rt_out, lf_out):
    for w in range(n_w):

        def rows(sl, w=w):
            for i in range(2):
                rt_out[i, w, sl, :] = plus(rt[i, w, sl, :], from_left[i, w, sl, :])
                rt_out[i + 2, w, sl, :] = rt[i + 2, w, sl, :]
                lf_out[i, w, sl, :] = lf[i, w, sl, :]
                lf_out[i + 2, w, sl, :] = plus(lf[i + 2, w, sl, :], from_right[i, w, sl, :])

        tiles_of(r, TILE, rows)


def join(rt, lf, from_left, from_right, after):
    return call(
        functools.partial(join_kernel, rt.shape[1], rt.shape[2]),
        (rt, lf, from_left, from_right),
        [VM] * 4,
        (sds(rt.shape, BF16),) * 2,
        (VM, VM),
        after=after,
    )


def turn_kernel(n_w, r, own, from_left, from_right, h1, h2, rt, lf, rest):
    half = r // 2

    def total(i, w, sl):
        return (
            own[i, w, sl, :].astype(F32) + from_left[i, w, sl, :].astype(F32) + from_right[i, w, sl, :].astype(F32)
        ).astype(BF16)

    for w in range(n_w):

        def rows(sl, w=w):
            h1[w, sl, :] = total(0, w, sl)
            h2[w, sl, :] = total(0, w, pl.ds(pl.multiple_of(sl.start + half, LANE), LANE))

        tiles_of(half, LANE, rows)

        def others(sl, w=w):
            for i, out in ((1, rt), (2, lf), (3, rest)):
                out[w, sl, :] = total(i, w, sl)

        tiles_of(r, TILE, others)


def turn(own, from_left, from_right, after):
    _, n_w, r, _ = own.shape
    half, full = sds((n_w, r // 2, LANE), BF16), sds((n_w, r, LANE), BF16)
    return call(
        functools.partial(turn_kernel, n_w, r),
        (own, from_left, from_right),
        [VM] * 3,
        (half, half, full, full, full),
        (VM,) * 5,
        after=after,
    )


def join_rows_kernel(n_w, r, rt, lf, from_left, from_right, rt_out, lf_out):
    half = r // 2
    for w in range(n_w):

        def rows(sl, w=w):
            up = pl.ds(pl.multiple_of(sl.start + half, LANE), LANE)
            rt_out[w, sl, :] = plus(rt[w, sl, :], from_left[w, sl, :])
            rt_out[w, up, :] = rt[w, up, :]
            lf_out[w, sl, :] = lf[w, sl, :]
            lf_out[w, up, :] = plus(lf[w, up, :], from_right[w, sl, :])

        tiles_of(half, LANE, rows)


def join_rows(rt, lf, from_left, from_right, after):
    return call(
        functools.partial(join_rows_kernel, rt.shape[0], rt.shape[1]),
        (rt, lf, from_left, from_right),
        [VM] * 4,
        (sds(rt.shape, BF16),) * 2,
        (VM, VM),
        after=after,
    )


def total3(refs, w, sl):
    return refs[0][w, sl, :].astype(F32) + refs[1][w, sl, :].astype(F32) + refs[2][w, sl, :].astype(F32)


def act_kernel(r, a, b, c, gates, ups, act):
    def rows(sl):
        gate = total3((a, b, c), 0, sl)
        up = total3((a, b, c), 1, sl)
        gates[sl, :] = gate
        ups[sl, :] = up
        act[sl, :] = (gate / (1.0 + jnp.exp(-gate)) * up).astype(BF16)

    tiles_of(r, LANE, rows)


def make_act(r, args, after):
    full = sds((r, LANE), F32)
    return call(
        functools.partial(act_kernel, r),
        args,
        [VM] * 3,
        (full, full, sds((r, LANE), BF16)),
        (VM,) * 3,
        after=after,
    )


def delta_kernel(r, gates, ups, wcol, a, b, c, out, sums):
    sums[...] = jnp.zeros_like(sums)

    def step(i, carry):
        sl = pl.ds(pl.multiple_of(i * LANE, LANE), LANE)
        gate = gates[sl, :]
        up = ups[sl, :]
        ag = total3((a, b, c), 0, sl)
        s = 1.0 / (1.0 + jnp.exp(-gate))
        silu = gate * s
        out[sl, :] = (ag * up * s * (1.0 + gate * (1.0 - s))).astype(BF16)
        out[pl.ds(pl.multiple_of(r + i * LANE, LANE), LANE), :] = (ag * silu).astype(BF16)
        act = (gate / (1.0 + jnp.exp(-gate)) * up).astype(BF16).astype(F32)
        w = wcol[sl, :]
        inner = act * ag * jnp.where(w > 0.0, 1.0 / jnp.maximum(w, 1e-6), 0.0)
        sums[pl.ds(i, 1), :] = jnp.sum(jnp.transpose(inner), axis=0, keepdims=True)
        return carry

    lax.fori_loop(0, r // LANE, step, 0)
    total = sums[...]
    hi = total.astype(BF16)
    out[2 * r : 2 * r + 16, :] = hi
    out[2 * r + 16 :, :] = (total - hi.astype(F32)).astype(BF16)


def make_deltas(r, args, after):
    (out,), tok = call(
        functools.partial(delta_kernel, r),
        args,
        [VM] * 6,
        (sds((2 * r + 32, LANE), BF16),),
        (VM,),
        [pltpu.VMEM((16, LANE), F32)],
        after,
    )
    return out, tok


def halves_kernel(n, from_left, from_right, h1, h2):
    h1[...] = from_left[:n]
    h2[...] = from_right[n:]


def halves(from_left, from_right, after):
    n = from_left.shape[0] // 2
    shape = sds((n, *from_left.shape[1:]), BF16)
    return call(
        functools.partial(halves_kernel, n), (from_left, from_right), [VM] * 2, (shape, shape), (VM, VM), after=after
    )


def line_kernel(n, own, from_right, from_left, o1, o2, out):
    out[0] = own[...]
    out[1] = from_right[...]
    out[2] = from_left[...]
    out[3, :n, :] = o1[...]
    out[3, n:, :] = o2[...]


def line(own, from_right, from_left, o1, o2, after):
    (out,), tok = call(
        functools.partial(line_kernel, o1.shape[0]),
        (own, from_right, from_left, o1, o2),
        [VM] * 5,
        (sds((4, *own.shape), BF16),),
        (VM,),
        after=after,
    )
    return out, tok


def stack_kernel(a, b, c, d, out):
    for j, v in enumerate((a, b, c, d)):
        out[j] = v[...]


def stack(vs, after):
    (out,), tok = call(stack_kernel, vs, [VM] * 4, (sds((4, *vs[0].shape), BF16),), (VM,), after=after)
    return out, tok


def down_kernel(nt, info, meta, w, wrow, pt, b0, br, bl, o1, o2, near, far, act, y, sems):
    r = nt * TILE
    copies = []
    for d, refs in ((0, (b0, b0, b0, b0)), (1, (br,) * 4), (-1, (bl,) * 4), (2, (o1, o1, o2, o2))):
        for j in range(4):
            at = j % 2 if d == 2 else j
            copies.append(
                pltpu.make_async_copy(
                    refs[j].at[at], act.at[:, lanes(block_at(info, ARRIVE[j], d))], sems.at[len(copies)]
                )
            )
    for cp in copies:
        cp.start()
    for cp in copies:
        cp.wait()
    tiles0 = meta[0]

    def tile_step(i, carry):
        rows = pl.ds(pl.multiple_of(i * TILE, TILE), TILE)
        e = (i >= tiles0).astype(jnp.int32)
        y[:, rows] = (dot_t(w[e], act[rows, :]) * wrow[:1, rows]).astype(BF16)
        return carry

    lax.fori_loop(0, nt, tile_step, 0)
    mix = dot(y[...], pt[...]).astype(BF16)
    for b in range(4):
        near[b] = mix[:, b * LANE : (b + 1) * LANE]
        far[b] = mix[:, (b + 4) * LANE : (b + 5) * LANE]


def down(nt, info, meta, w, wrow, pt, bufs, after):
    r = nt * TILE
    return call(
        functools.partial(down_kernel, nt),
        (info, meta, w, wrow, pt, *bufs),
        [SM, SM, VM, VM, VM] + [ANY] * 5,
        (sds((4, FEAT, LANE), BF16), sds((4, FEAT, LANE), BF16), sds((r, HID), BF16)),
        (VM, VM, VM),
        [pltpu.VMEM((FEAT, r), BF16), pltpu.SemaphoreType.DMA((16,))],
        after,
    )


def dgrad_kernel(r, meta, ge, act, dgrad, tail):
    off = pl.multiple_of(meta[0] * TILE, TILE)
    for n in range(HID // 512):
        cols = slice(n * 512, (n + 1) * 512)
        tail[:r, :] = act[:, cols]
        if r < PAD:
            tail[r:, :] = jnp.zeros((PAD - r, 512), BF16)
        dgrad[0, :, cols] = dot(ge[0], tail[:SPAN, :]).astype(BF16)
        dgrad[1, :, cols] = dot(ge[1], tail[pl.ds(off, SPAN), :]).astype(BF16)


def down_grads(r, meta, ge, act, after):
    return call(
        functools.partial(dgrad_kernel, r),
        (meta, ge, act),
        [SM, VM, VM],
        (sds((2, FEAT, HID), BF16),),
        (VM,),
        [pltpu.VMEM((PAD, 512), BF16)],
        after,
    )


def line_blocks(bufs, d):
    if d == 2:
        return [(bufs[j // 2], j % 2, ARRIVE[j]) for j in range(4)]
    return [(bufs[0], j, ARRIVE[j]) for j in range(4)]


def wgrad_kernel(r, d, n_buf, fresh, info, meta, xe, *refs):
    blocks = line_blocks(refs[:n_buf], d)
    refs = refs[n_buf:] if fresh else refs[n_buf + 2 :]
    outs, (land, stage, in_sems, out_sems) = refs[:2], refs[2:]
    off = pl.multiple_of(meta[0] * TILE, TILE)
    fetch = [
        [
            pltpu.make_async_copy(
                ref.at[at, pl.ds(a * r, r), :],
                land.at[a, pl.ds(0, r), pl.ds(j * LANE, LANE)],
                in_sems.at[a * 4 + j],
            )
            for j, (ref, at, _) in enumerate(blocks)
        ]
        for a in range(2)
    ]
    store = [
        [
            pltpu.make_async_copy(
                stage.at[a, :, :, pl.ds(j * LANE, LANE)],
                outs[a].at[:, :, lanes(block_at(info, inner, d))],
                out_sems.at[a * 4 + j],
            )
            for j, (_, _, inner) in enumerate(blocks)
        ]
        for a in range(2)
    ]
    for cps in fetch:
        for cp in cps:
            cp.start()
    if r < PAD:
        land[:, r:, :] = jnp.zeros((2, PAD - r, 512), BF16)
    for a in range(2):
        for cp in fetch[a]:
            cp.wait()
        stage[a, 0] = dot(xe[0], land[a, :SPAN, :]).astype(BF16)
        stage[a, 1] = dot(xe[1], land[a, pl.ds(off, SPAN), :]).astype(BF16)
        for cp in store[a]:
            cp.start()
    for cps in store:
        for cp in cps:
            cp.wait()


def wgrad(r, d, info, meta, xe, bufs, prev, after):
    shape = sds((2, FEAT, HID), BF16)
    args = [info, meta, xe, *bufs]
    alias = {}
    if prev is not None:
        alias = {len(args): 0, len(args) + 1: 1}
        args += list(prev)
    return call(
        functools.partial(wgrad_kernel, r, d, len(bufs), prev is None),
        args,
        [SM, SM, VM] + [ANY] * (len(args) - 3),
        (shape, shape),
        (ANY, ANY),
        [
            pltpu.VMEM((2, PAD, 512), BF16),
            pltpu.VMEM((2, 2, FEAT, 512), BF16),
            pltpu.SemaphoreType.DMA((8,)),
            pltpu.SemaphoreType.DMA((8,)),
        ],
        after,
        alias=alias,
    )


def back_kernel(nt, d, n_buf, first, last, info, meta, *refs):
    r = nt * TILE
    refs = list(refs)
    prev = None if first else (refs.pop(0), refs.pop(0))
    pt = refs.pop(0) if last else None
    blocks = line_blocks(refs[:n_buf], d)
    ws = refs[n_buf : n_buf + 2]
    outs, (land, wl, tails, sems, w_sems, t_sems) = refs[n_buf + 2 : n_buf + 4], refs[-6:]
    acc, inner = refs[n_buf + 4 : n_buf + 6] if last else outs
    tiles0 = meta[0]
    fetch = [
        [
            pltpu.make_async_copy(
                ref.at[at, pl.ds(a * r, r), :], land.at[a, :, pl.ds(j * LANE, LANE)], sems.at[a * 4 + j]
            )
            for j, (ref, at, _) in enumerate(blocks)
        ]
        + [
            pltpu.make_async_copy(
                ws[a].at[:, :, lanes(block_at(info, in_, d))],
                wl.at[a, :, :, pl.ds(j * LANE, LANE)],
                w_sems.at[a * 4 + j],
            )
            for j, (_, _, in_) in enumerate(blocks)
        ]
        for a in range(2)
    ]
    sums = [
        pltpu.make_async_copy(ref.at[at, pl.ds(2 * r, 32), :], tails.at[j], t_sems.at[j])
        for j, (ref, at, _) in enumerate(blocks)
    ]
    for cp in fetch[0] + fetch[1] + sums:
        cp.start()
    for cp in sums:
        cp.wait()
    s_now = jnp.zeros((16, LANE), F32) if first else prev[1][...]
    for j in range(4):
        s_now = s_now + (tails[j, :16, :].astype(F32) + tails[j, 16:, :].astype(F32))
    inner[...] = s_now
    for a in range(2):
        for cp in fetch[a]:
            cp.wait()

    def step(i, carry):
        rows = pl.ds(pl.multiple_of(i * TILE, TILE), TILE)
        e = (i >= tiles0).astype(jnp.int32)
        now = dot_t(wl[0, e], land[0, rows, :]) + dot_t(wl[1, e], land[1, rows, :])
        acc[:, rows] = now if first else prev[0][:, rows] + now
        return carry

    lax.fori_loop(0, nt, step, 0, unroll=nt == 5)
    if last:
        near, far = outs
        total = dot(acc[...].astype(BF16), pt[...]).astype(BF16)
        s3 = jnp.concatenate(split3(s_now), axis=0)
        wide = jnp.concatenate([s3] * (r // LANE), axis=1)
        at_row = lax.broadcasted_iota(jnp.int32, (48, r), 0)
        at_row = at_row - (at_row // 16) * 16
        keep = at_row == lax.broadcasted_iota(jnp.int32, (48, r), 1) // LANE
        got = dot(jnp.where(keep, wide, jnp.zeros_like(wide)), pt[...])
        got = (got[:16] + got[16:32]) + got[32:]
        second = lax.broadcasted_iota(jnp.int32, (16, TOKS), 0) >= 2 * tiles0
        dense0 = jnp.sum(jnp.where(second, 0.0, got), axis=0, keepdims=True)
        dense1 = jnp.sum(jnp.where(second, got, 0.0), axis=0, keepdims=True)
        expert = lax.broadcasted_iota(jnp.int32, (16, TOKS), 0)
        at = info[1] * 2
        table = jnp.where(expert == at, dense0, 0.0) + jnp.where(expert == at + 1, dense1, 0.0)
        t3 = split3(table)
        for b in range(8):
            cols = slice(b * LANE, (b + 1) * LANE)
            out = (near if b < 4 else far).at[b % 4]
            out[:FEAT, :] = total[:, cols]
            for q in range(3):
                out[FEAT + 16 * q : FEAT + 16 * (q + 1), :] = t3[q][:, cols]


def back(nt, d, info, meta, bufs, wg, wu, prev, pt, after):
    r = nt * TILE
    first, last = prev is None, pt is not None
    args = [info, meta]
    specs = [SM, SM]
    if not first:
        args += list(prev)
        specs += [VM, VM]
    if last:
        args.append(pt)
        specs.append(VM)
    args += [*bufs, wg, wu]
    specs += [ANY] * (len(bufs) + 2)
    keep = [((FEAT, r), F32), ((16, LANE), F32)]
    scratch = [
        pltpu.VMEM((2, r, 512), BF16),
        pltpu.VMEM((2, 2, FEAT, 512), BF16),
        pltpu.VMEM((4, 32, LANE), BF16),
        pltpu.SemaphoreType.DMA((8,)),
        pltpu.SemaphoreType.DMA((8,)),
        pltpu.SemaphoreType.DMA((4,)),
    ]
    if last:
        out_shape = (sds((4, FEAT + 48, LANE), BF16),) * 2
        scratch = [pltpu.VMEM(*k) for k in keep] + scratch
    else:
        out_shape = tuple(sds(*k) for k in keep)
    return call(
        functools.partial(back_kernel, nt, d, len(bufs), first, last),
        args,
        specs,
        out_shape,
        (VM, VM),
        scratch,
        after,
    )


def home_kernel(own, other, ids, tg, wg):
    total = own[...].astype(F32)
    for j in range(3):
        total = total + other[j][...].astype(F32)
    tg[...] = total[:FEAT].astype(BF16)
    dense = (total[FEAT : FEAT + 16] + total[FEAT + 16 : FEAT + 32]) + total[FEAT + 32 :]
    expert = lax.broadcasted_iota(jnp.int32, (16, LANE), 0)
    for k in range(8):
        wg[k : k + 1, :] = jnp.sum(jnp.where(expert == ids[k : k + 1, :], dense, 0.0), axis=0, keepdims=True)


def home(own, a, b, c, ids):
    def kern(own, a, b, c, ids, tg, wg):
        home_kernel(own, (a, b, c), ids, tg, wg)

    return pl.pallas_call(
        kern,
        out_shape=(sds((FEAT, LANE), BF16), sds((8, LANE), F32)),
        in_specs=[VM] * 5,
        out_specs=(VM, VM),
    )(own, a, b, c, ids)


def to_experts(v):
    return [v] + [z_shift(v, -k) for k in (1, 2, 3)]


def first_stack_kernel(a, b, c, d, og, out, og_out):
    for j, v in enumerate((a, b, c, d)):
        out[j] = v[...]
    og_out[...] = og[...]


def near_kernel(near, there, *outs):
    for j in range(4):
        outs[j][...] = plus(near[j], there[j])


def to_home(near, far, after):
    there = mate(far)
    mine, tok = call(near_kernel, (near, there), [VM, VM], (sds(near.shape[1:], BF16),) * 4, (VM,) * 4, after=after)
    return [mine[0]] + [z_shift(mine[k], k) for k in (1, 2, 3)], tok


def mixed_kernel(a, b, c, d, out):
    out[...] = ((a[...].astype(F32) + b[...].astype(F32)) + (c[...].astype(F32) + d[...].astype(F32))).astype(BF16)


def both(to_right, to_left, phase):
    return hop(to_right, phase, 1), hop(to_left, phase, -1)


def passes(nt, info, ids, packed, og, w_gate, w_up, w_down):
    r = nt * TILE
    (mine, og), tok = call(
        first_stack_kernel,
        (*to_experts(packed), og),
        [VM] * 5,
        (sds((4, FEAT + 48, LANE), BF16), sds((FEAT, LANE), BF16)),
        (VM, VM),
    )
    other = mate(mine)
    og_line = to_experts(og)
    (xr, pt, wcol, wrow, meta), tok = make_rows(nt, info, mine, other, (tok,))
    gu, dn = (w_gate, w_up), (w_down,)
    og_mine, tok = stack(og_line, (tok,))
    (g1, g2), tok = parts(nt, (2,), True, info, meta, xr, gu, (tok,))
    g_in = both(g1, g2, 0)
    og_other = mate(og_mine)
    (gr, xe, ge), tok = make_grads(nt, meta, og_mine, og_other, xr, pt, wcol, (tok,))
    (a1, a2), tok = parts(nt, (2,), True, info, meta, gr, dn, (tok,))
    a_in = both(a1, a2, 0)
    (g_rt, g_lf), tok = parts(nt, (1, -1), False, info, meta, xr, gu, (tok,))
    (g_rt, g_lf), tok = join(g_rt, g_lf, *g_in, (tok, *a_in))
    g_in = both(g_rt, g_lf, 0)
    (a_rt, a_lf), tok = parts(nt, (1, -1), False, info, meta, gr, dn, (tok,))
    (a_rt, a_lf), tok = join(a_rt, a_lf, *a_in, (tok,))
    a_in = both(a_rt, a_lf, 0)
    (g_own,), tok = parts(nt, (0,), False, info, meta, xr, gu, (tok,))
    (a_own,), tok = parts(nt, (0,), False, info, meta, gr, dn, (tok,))
    (h1, h2, g_rt, g_lf, g_own), tok = turn(g_own, *g_in, (tok,))
    g_in = both(h1, h2, 1)
    (g_rt, g_lf), tok = join_rows(g_rt, g_lf, *g_in, (tok,))
    g_in = both(g_rt, g_lf, 1)
    (h1, h2, a_rt, a_lf, a_own), tok = turn(a_own, *a_in, (tok,))
    a_in = both(h1, h2, 1)
    (gates, ups, act), tok = make_act(r, (g_own, *g_in), (tok,))
    c_in = both(act, act, 0)
    (a_rt, a_lf), tok = join_rows(a_rt, a_lf, *a_in, (tok,))
    a_in = both(a_rt, a_lf, 1)
    (h1, h2), tok = halves(*c_in, (tok,))
    c_far = both(h1, h2, 0)
    c_line, tok = line(act, c_in[1], c_in[0], *c_far, (tok,))
    c_left, c_right = both(c_line, c_line, 1)
    delta, tok = make_deltas(r, (gates, ups, wcol, a_own, *a_in), (tok,))
    d_in = both(delta, delta, 0)
    (h1, h2), tok = halves(c_left, c_right, (tok,))
    c_far = both(h1, h2, 1)
    (h1, h2), tok = halves(*d_in, (tok,))
    d_far = both(h1, h2, 0)
    d_line, tok = line(delta, d_in[1], d_in[0], *d_far, (tok, *c_far))
    d_left, d_right = both(d_line, d_line, 1)

    def back_of(d, bufs, acc, table):
        return back(nt, d, info, meta, bufs, w_gate, w_up, acc, table, (tok,))

    def wgrad_of(d, bufs, prev):
        return wgrad(r, d, info, meta, xe, bufs, prev, (tok,))

    (near, far, act_all), tok = down(nt, info, meta, w_down, wrow, pt, (c_line, c_right, c_left, *c_far), (tok,))
    acc, tok = back_of(0, (d_line,), None, None)
    mixed_home, tok = to_home(near, far, (tok,))
    grads, tok = wgrad_of(0, (d_line,), None)
    (down_grad,), tok = down_grads(r, meta, ge, act_all, (tok,))
    (mixed,), tok = call(mixed_kernel, mixed_home, [VM] * 4, (sds((FEAT, LANE), BF16),), (VM,), after=(tok,))
    (h1, h2), tok = halves(d_left, d_right, (tok,))
    d_far = both(h1, h2, 1)
    acc, tok = back_of(1, (d_right,), acc, None)
    acc, tok = back_of(-1, (d_left,), acc, None)
    grads, tok = wgrad_of(1, (d_right,), grads)
    grads, tok = wgrad_of(-1, (d_left,), grads)
    (near, far), tok = back_of(2, d_far, acc, pt)
    token_home, _ = to_home(near, far, ())
    (gate_grad, up_grad), tok = wgrad_of(2, d_far, grads)
    token_grad, weight_grad = home(*token_home, ids)
    return meta[2], (mixed, token_grad, weight_grad, gate_grad, up_grad, down_grad)


def body(tokens, expert_ids, route_weights, output_grad, w_gate, w_up, w_down):
    info = jnp.stack([lax.axis_index("ctx"), lax.axis_index("exp")]).astype(jnp.int32)
    ids = expert_ids.T
    og = output_grad.T
    weights = (w_gate, w_up, w_down.transpose(0, 2, 1))
    packed = pack(tokens.T, ids, route_weights.T)
    most, outs = passes(5, info, ids, packed, og, *weights)

    def again(state):
        return jnp.zeros_like(state[0]), passes(6, info, ids, packed, og, *weights)[1]

    _, outs = lax.while_loop(lambda state: state[0] > 5, again, (most, outs))
    mixed, token_grad, weight_grad, gate_grad, up_grad, down_grad = outs
    return (
        mixed.T,
        token_grad.T,
        weight_grad.T,
        gate_grad,
        up_grad,
        down_grad.transpose(0, 2, 1),
    )


def solution(mesh):
    return jax.shard_map(
        body,
        mesh=mesh,
        in_specs=(
            P("exp", "ctx"),
            P("exp", None),
            P("exp", None),
            P("exp", "ctx"),
            P("exp", "ctx", None),
            P("exp", "ctx", None),
            P("exp", None, "ctx"),
        ),
        out_specs=(
            P("exp", "ctx"),
            P("exp", "ctx"),
            P("exp", None),
            P("exp", "ctx", None),
            P("exp", "ctx", None),
            P("exp", None, "ctx"),
        ),
        check_vma=False,
    )
```

```python
import functools

import jax
import jax.numpy as jnp
from jax import lax
from jax.experimental import pallas as pl
from jax.experimental.pallas import tpu as pltpu
from jax.sharding import PartitionSpec as P

F32 = jnp.float32
BF16 = jnp.bfloat16
TILE = 256
LANE = 128
FEAT = 448
HID = 2048
SPAN = 768
PAD = 2 * SPAN
LEAVE = (2, 1, -1, 0)
ARRIVE = (0, 1, -1, 2)
TOKS = 1024
BOTH = ("ctx", "exp")
VM = pl.BlockSpec(memory_space=pltpu.VMEM)
SM = pl.BlockSpec(memory_space=pltpu.SMEM)
ANY = pl.BlockSpec(memory_space=pl.ANY)


def params(mib):
    return pltpu.CompilerParams(vmem_limit_bytes=mib * 1024 * 1024)


def sds(shape, dtype):
    return jax.ShapeDtypeStruct(shape, dtype)


def call(kern, args, specs, out_shape, out_specs, scratch=(), after=(), mib=32, alias=None):
    n_in, n_out = len(args), len(out_shape)
    skip = n_in + len(after)

    def wrapped(*refs):
        kern(*refs[:n_in], *refs[skip : skip + n_out], *refs[skip + n_out + 1 :])

    res = pl.pallas_call(
        wrapped,
        out_shape=(*out_shape, sds((8, LANE), F32)),
        in_specs=[*specs] + [ANY] * len(after),
        out_specs=(*out_specs, ANY),
        scratch_shapes=list(scratch),
        input_output_aliases=alias or {},
        compiler_params=params(mib),
        cost_estimate=pl.CostEstimate(flops=1, bytes_accessed=1, transcendentals=0),
    )(*args, *after)
    return res[:-1], res[-1]


def dot(a, b):
    return lax.dot_general(a, b, (((1,), (0,)), ((), ())), preferred_element_type=F32)


def dot_t(a, b):
    return lax.dot_general(a, b, (((1,), (1,)), ((), ())), preferred_element_type=F32)


def hop(v, phase, step):
    pairs = []
    for y in range(4):
        for x in range(4):
            for e in range(8):
                along_x = (e % 2 == 0) == (phase == 0)
                to = (y * 4 + (x + step) % 4) if along_x else (((y + step) % 4) * 4 + x)
                pairs.append(((y * 4 + x) * 8 + e, to * 8 + e))
    return lax.ppermute(v, BOTH, pairs)


def z_shift(v, k):
    return lax.ppermute(v, "exp", [(z * 2 + c, ((z + k) % 4) * 2 + c) for z in range(4) for c in range(2)])


def mate(v):
    return lax.ppermute(v, "exp", [(e, e ^ 1) for e in range(8)])


def block_at(info, d0, d1):
    ctx = info[0]
    y = ctx // 4
    x = ctx - y * 4
    odd = info[1] - (info[1] // 2) * 2
    dx = d0 + odd * (d1 - d0)
    dy = d1 + odd * (d0 - d1)
    return jnp.bitwise_and(y + dy + 8, 3) * 4 + jnp.bitwise_and(x + dx + 8, 3)


def lanes(c):
    return pl.ds(pl.multiple_of(c * LANE, LANE), LANE)


def pack_kernel(tok, ids, rw, out):
    out[:FEAT, :] = tok[...]
    expert = lax.broadcasted_iota(jnp.int32, (16, LANE), 0)
    dense = jnp.zeros((16, LANE), F32)
    for k in range(8):
        dense += jnp.where(ids[k : k + 1, :] == expert, rw[k : k + 1, :], 0.0)
    for i, part in enumerate(split3(dense)):
        out[FEAT + 16 * i : FEAT + 16 * (i + 1), :] = part


def split3(v):
    hi = v.astype(BF16)
    rest = v - hi.astype(F32)
    mid = rest.astype(BF16)
    low = (rest - mid.astype(F32)).astype(BF16)
    return hi, mid, low


def pack(tok, ids, rw):
    return pl.pallas_call(pack_kernel, out_shape=sds((FEAT + 48, LANE), BF16), in_specs=[VM] * 3, out_specs=VM)(
        tok, ids, rw
    )


def rows_kernel(nt, info, mine, other, xr, pt, wcol, wrow, meta, tt_out):
    blocks = [mine[j] for j in range(4)] + [other[j] for j in range(4)]
    tt = jnp.concatenate([b[:FEAT, :] for b in blocks], axis=1)
    expert = lax.broadcasted_iota(jnp.int32, (16, LANE), 0)
    first = info[1] * 2
    weights = [[], []]
    named = jnp.zeros((16, 1), F32)
    for b in blocks:
        tail = b[FEAT : FEAT + 48, :].astype(F32)
        dense = (tail[:16] + tail[16:32]) + tail[32:48]
        named += jnp.sum((dense > 0.0).astype(F32), axis=1, keepdims=True)
        for l in range(2):
            weights[l].append(jnp.sum(jnp.where(expert == first + l, dense, 0.0), axis=0, keepdims=True))
    member = [[(w > 0.0).astype(F32) for w in ws] for ws in weights]
    before = (
        lax.broadcasted_iota(jnp.int32, (LANE, LANE), 0) < lax.broadcasted_iota(jnp.int32, (LANE, LANE), 1)
    ).astype(BF16)
    ranks = dot(jnp.concatenate(member[0] + member[1], axis=0).astype(BF16), before)
    slots = []
    base = jnp.zeros((1, 1), F32)
    for l in range(2):
        run = base
        for b in range(8):
            m = member[l][b]
            slots.append(jnp.where(m > 0.0, ranks[l * 8 + b : l * 8 + b + 1, :] + run, -1.0))
            run = run + jnp.sum(m, axis=1, keepdims=True)
        if l == 0:
            base = jnp.maximum(jnp.floor((run + (TILE - 1.0)) * (1.0 / TILE)), 1.0) * TILE
    count = jnp.sum(jnp.concatenate(member[0], axis=0)).astype(jnp.int32)
    meta[0] = jnp.maximum((count + (TILE - 1)) // TILE, 1)
    count = jnp.sum(jnp.concatenate(member[1], axis=0)).astype(jnp.int32)
    meta[1] = jnp.maximum((count + (TILE - 1)) // TILE, 1)
    tiles = jnp.broadcast_to(jnp.maximum(jnp.floor((named + (TILE - 1.0)) * (1.0 / TILE)), 1.0), (16, LANE))
    even = lax.broadcasted_iota(jnp.int32, (16, 16), 0) // 2 == lax.broadcasted_iota(jnp.int32, (16, 16), 1) // 2
    most = jnp.max(dot(even.astype(BF16), tiles.astype(BF16))).astype(jnp.int32)
    meta[2] = most
    tt_out[...] = tt
    q0 = jnp.concatenate(slots[:8], axis=1).astype(jnp.int32)
    q1 = jnp.concatenate(slots[8:], axis=1).astype(jnp.int32)
    w0 = jnp.concatenate(weights[0], axis=1)
    w1 = jnp.concatenate(weights[1], axis=1)

    def tile_rows(i, carry):
        sl = pl.ds(pl.multiple_of(i * TILE, TILE), TILE)
        row = lax.broadcasted_iota(jnp.int32, (TILE, TOKS), 0) + i * TILE
        hit0, hit1 = row == q0, row == q1
        one = jnp.where(hit0 | hit1, 1.0, 0.0).astype(BF16)
        pt[sl, :] = one
        col = jnp.sum(jnp.where(hit0, w0, 0.0) + jnp.where(hit1, w1, 0.0), axis=1, keepdims=True)
        wide = jnp.broadcast_to(col, (TILE, LANE))
        wcol[sl, :] = wide
        wrow[:, sl] = jnp.transpose(wide)[:8, :]
        xr[sl, :] = dot_t(one, tt_out[...]).astype(BF16)
        return carry

    lax.fori_loop(0, nt, tile_rows, 0)


def make_rows(nt, info, mine, other, after):
    r = nt * TILE
    return call(
        functools.partial(rows_kernel, nt),
        (info, mine, other),
        [SM, VM, VM],
        (
            sds((r, FEAT), BF16),
            sds((r, TOKS), BF16),
            sds((r, LANE), F32),
            sds((8, r), F32),
            sds((8,), jnp.int32),
        ),
        (VM, VM, VM, VM, SM),
        [pltpu.VMEM((FEAT, TOKS), BF16)],
        after,
    )


def grads_kernel(nt, meta, mine, other, xr, pt, wcol, gr, xe, ge, gg, turned):
    r = nt * TILE
    off = pl.multiple_of(meta[0] * TILE, TILE)
    for j in range(4):
        gg[:, j * LANE : (j + 1) * LANE] = mine[j]
        gg[:, (j + 4) * LANE : (j + 5) * LANE] = other[j]
    if r < PAD:
        turned[:, :, r:] = jnp.zeros((2, FEAT, PAD - r), BF16)

    def tile_step(i, carry):
        sl = pl.ds(pl.multiple_of(i * TILE, TILE), TILE)
        g = (dot_t(pt[sl, :], gg[...]) * wcol[sl, :1]).astype(BF16)
        gr[sl, :] = g
        turned[0, :, sl] = jnp.transpose(xr[sl, :])
        turned[1, :, sl] = jnp.transpose(g)
        return carry

    lax.fori_loop(0, nt, tile_step, 0, unroll=nt == 5)
    mine_too = lax.broadcasted_iota(jnp.int32, (FEAT, SPAN), 1) < off
    zero = jnp.zeros((FEAT, SPAN), BF16)
    for q, out in ((0, xe), (1, ge)):
        out[0] = jnp.where(mine_too, turned[q, :, :SPAN], zero)
        out[1] = turned[q, :, pl.ds(off, SPAN)]


def make_grads(nt, meta, mine, other, xr, pt, wcol, after):
    r = nt * TILE
    span = sds((2, FEAT, SPAN), BF16)
    return call(
        functools.partial(grads_kernel, nt),
        (meta, mine, other, xr, pt, wcol),
        [SM] + [VM] * 5,
        (sds((r, FEAT), BF16), span, span),
        (VM, VM, VM),
        [pltpu.VMEM((FEAT, TOKS), BF16), pltpu.VMEM((2, FEAT, PAD), BF16)],
        after,
    )


def parts_kernel(nt, outers, split, n_w, info, meta, src, *refs):
    weights, refs = refs[:n_w], refs[n_w:]
    n_out = len(outers) * (2 if split else 1)
    outs, (bufs, sems) = refs[:n_out], refs[n_out:]
    jobs = [(p, w) for p in range(len(outers)) for w in range(n_w)]
    copies = [
        [
            pltpu.make_async_copy(
                weights[w].at[:, :, lanes(block_at(info, outers[p], LEAVE[i]))],
                bufs.at[n, :, :, pl.ds(i * LANE, LANE)],
                sems.at[n * 4 + i],
            )
            for i in range(4)
        ]
        for n, (p, w) in enumerate(jobs)
    ]
    for cps in copies:
        for cp in cps:
            cp.start()
    tiles0 = meta[0]
    for n, (p, w) in enumerate(jobs):
        for cp in copies[n]:
            cp.wait()

        def tile_step(t, carry, n=n, p=p, w=w):
            sl = pl.ds(pl.multiple_of(t * TILE, TILE), TILE)
            e = (t >= tiles0).astype(jnp.int32)
            out = dot(src[sl, :], bufs[n, e]).astype(BF16)
            for i in range(4):
                o, at = (outs[2 * p + i // 2], i % 2) if split else (outs[p], i)
                o[at, w, sl, :] = out[:, i * LANE : (i + 1) * LANE]
            return carry

        lax.fori_loop(0, nt, tile_step, 0, unroll=nt == 5)


def parts(nt, outers, split, info, meta, src, weights, after):
    n_w = len(weights)
    shape = sds((2 if split else 4, n_w, nt * TILE, LANE), BF16)
    n_out = len(outers) * (2 if split else 1)
    return call(
        functools.partial(parts_kernel, nt, outers, split, n_w),
        (info, meta, src, *weights),
        [SM, SM, VM] + [ANY] * n_w,
        (shape,) * n_out,
        (VM,) * n_out,
        [
            pltpu.VMEM((len(outers) * n_w, 2, FEAT, 512), BF16),
            pltpu.SemaphoreType.DMA((4 * len(outers) * n_w,)),
        ],
        after,
    )


def tiles_of(n, size, body):
    def step(i, carry):
        body(pl.ds(pl.multiple_of(i * size, size), size))
        return carry

    lax.fori_loop(0, n // size, step, 0)


def plus(a, b):
    return (a.astype(F32) + b.astype(F32)).astype(BF16)


def join_kernel(n_w, r, rt, lf, from_left, from_right, rt_out, lf_out):
    for w in range(n_w):

        def rows(sl, w=w):
            for i in range(2):
                rt_out[i, w, sl, :] = plus(rt[i, w, sl, :], from_left[i, w, sl, :])
                rt_out[i + 2, w, sl, :] = rt[i + 2, w, sl, :]
                lf_out[i, w, sl, :] = lf[i, w, sl, :]
                lf_out[i + 2, w, sl, :] = plus(lf[i + 2, w, sl, :], from_right[i, w, sl, :])

        tiles_of(r, TILE, rows)


def join(rt, lf, from_left, from_right, after):
    return call(
        functools.partial(join_kernel, rt.shape[1], rt.shape[2]),
        (rt, lf, from_left, from_right),
        [VM] * 4,
        (sds(rt.shape, BF16),) * 2,
        (VM, VM),
        after=after,
    )


def gate(vs, after):
    return call(
        lambda *refs: None,
        vs,
        [ANY] * len(vs),
        tuple(sds(v.shape, v.dtype) for v in vs),
        (ANY,) * len(vs),
        after=after,
        alias={i: i for i in range(len(vs))},
    )


def turn_kernel(n_w, r, own, from_left, from_right, h1, h2, rt, lf, rest):
    half = r // 2

    def total(i, w, sl):
        return (
            own[i, w, sl, :].astype(F32) + from_left[i, w, sl, :].astype(F32) + from_right[i, w, sl, :].astype(F32)
        ).astype(BF16)

    for w in range(n_w):

        def rows(sl, w=w):
            h1[w, sl, :] = total(0, w, sl)
            h2[w, sl, :] = total(0, w, pl.ds(pl.multiple_of(sl.start + half, LANE), LANE))

        tiles_of(half, LANE, rows)

        def others(sl, w=w):
            for i, out in ((1, rt), (2, lf), (3, rest)):
                out[w, sl, :] = total(i, w, sl)

        tiles_of(r, TILE, others)


def turn(own, from_left, from_right, after):
    _, n_w, r, _ = own.shape
    half, full = sds((n_w, r // 2, LANE), BF16), sds((n_w, r, LANE), BF16)
    return call(
        functools.partial(turn_kernel, n_w, r),
        (own, from_left, from_right),
        [VM] * 3,
        (half, half, full, full, full),
        (VM,) * 5,
        after=after,
    )


def join_rows_kernel(n_w, r, rt, lf, from_left, from_right, rt_out, lf_out):
    half = r // 2
    for w in range(n_w):

        def rows(sl, w=w):
            up = pl.ds(pl.multiple_of(sl.start + half, LANE), LANE)
            rt_out[w, sl, :] = plus(rt[w, sl, :], from_left[w, sl, :])
            rt_out[w, up, :] = rt[w, up, :]
            lf_out[w, sl, :] = lf[w, sl, :]
            lf_out[w, up, :] = plus(lf[w, up, :], from_right[w, sl, :])

        tiles_of(half, LANE, rows)


def join_rows(rt, lf, from_left, from_right, after):
    return call(
        functools.partial(join_rows_kernel, rt.shape[0], rt.shape[1]),
        (rt, lf, from_left, from_right),
        [VM] * 4,
        (sds(rt.shape, BF16),) * 2,
        (VM, VM),
        after=after,
    )


def total3(refs, w, sl):
    return refs[0][w, sl, :].astype(F32) + refs[1][w, sl, :].astype(F32) + refs[2][w, sl, :].astype(F32)


def act_kernel(r, a, b, c, gates, ups, act):
    def rows(sl):
        gate = total3((a, b, c), 0, sl)
        up = total3((a, b, c), 1, sl)
        gates[sl, :] = gate
        ups[sl, :] = up
        act[sl, :] = (gate / (1.0 + jnp.exp(-gate)) * up).astype(BF16)

    tiles_of(r, LANE, rows)


def make_act(r, args, after):
    full = sds((r, LANE), F32)
    return call(
        functools.partial(act_kernel, r),
        args,
        [VM] * 3,
        (full, full, sds((r, LANE), BF16)),
        (VM,) * 3,
        after=after,
    )


def delta_kernel(r, gates, ups, wcol, a, b, c, out, sums):
    sums[...] = jnp.zeros_like(sums)

    def step(i, carry):
        sl = pl.ds(pl.multiple_of(i * LANE, LANE), LANE)
        gate = gates[sl, :]
        up = ups[sl, :]
        ag = total3((a, b, c), 0, sl)
        s = 1.0 / (1.0 + jnp.exp(-gate))
        silu = gate * s
        out[sl, :] = (ag * up * s * (1.0 + gate * (1.0 - s))).astype(BF16)
        out[pl.ds(pl.multiple_of(r + i * LANE, LANE), LANE), :] = (ag * silu).astype(BF16)
        act = (gate / (1.0 + jnp.exp(-gate)) * up).astype(BF16).astype(F32)
        w = wcol[sl, :]
        inner = act * ag * jnp.where(w > 0.0, 1.0 / jnp.maximum(w, 1e-6), 0.0)
        sums[pl.ds(i, 1), :] = jnp.sum(jnp.transpose(inner), axis=0, keepdims=True)
        return carry

    lax.fori_loop(0, r // LANE, step, 0)
    total = sums[...]
    hi = total.astype(BF16)
    out[2 * r : 2 * r + 16, :] = hi
    out[2 * r + 16 :, :] = (total - hi.astype(F32)).astype(BF16)


def make_deltas(r, args, after):
    (out,), tok = call(
        functools.partial(delta_kernel, r),
        args,
        [VM] * 6,
        (sds((2 * r + 32, LANE), BF16),),
        (VM,),
        [pltpu.VMEM((16, LANE), F32)],
        after,
    )
    return out, tok


def halves_kernel(n, from_left, from_right, h1, h2):
    h1[...] = from_left[:n]
    h2[...] = from_right[n:]


def halves(from_left, from_right, after):
    n = from_left.shape[0] // 2
    shape = sds((n, *from_left.shape[1:]), BF16)
    return call(
        functools.partial(halves_kernel, n), (from_left, from_right), [VM] * 2, (shape, shape), (VM, VM), after=after
    )


def line_kernel(n, own, from_right, from_left, o1, o2, out):
    out[0] = own[...]
    out[1] = from_right[...]
    out[2] = from_left[...]
    out[3, :n, :] = o1[...]
    out[3, n:, :] = o2[...]


def line(own, from_right, from_left, o1, o2, after):
    (out,), tok = call(
        functools.partial(line_kernel, o1.shape[0]),
        (own, from_right, from_left, o1, o2),
        [VM] * 5,
        (sds((4, *own.shape), BF16),),
        (VM,),
        after=after,
    )
    return out, tok


def stack_kernel(a, b, c, d, out):
    for j, v in enumerate((a, b, c, d)):
        out[j] = v[...]


def stack(vs, after):
    (out,), tok = call(stack_kernel, vs, [VM] * 4, (sds((4, *vs[0].shape), BF16),), (VM,), after=after)
    return out, tok


def down_kernel(nt, info, meta, w, wrow, pt, b0, br, bl, o1, o2, near, far, act, y, sems):
    r = nt * TILE
    copies = []
    for d, refs in ((0, (b0, b0, b0, b0)), (1, (br,) * 4), (-1, (bl,) * 4), (2, (o1, o1, o2, o2))):
        for j in range(4):
            at = j % 2 if d == 2 else j
            copies.append(
                pltpu.make_async_copy(
                    refs[j].at[at], act.at[:, lanes(block_at(info, ARRIVE[j], d))], sems.at[len(copies)]
                )
            )
    for cp in copies:
        cp.start()
    for cp in copies:
        cp.wait()
    tiles0 = meta[0]

    def tile_step(i, carry):
        rows = pl.ds(pl.multiple_of(i * TILE, TILE), TILE)
        e = (i >= tiles0).astype(jnp.int32)
        y[:, rows] = (dot_t(w[e], act[rows, :]) * wrow[:1, rows]).astype(BF16)
        return carry

    lax.fori_loop(0, nt, tile_step, 0)
    mix = dot(y[...], pt[...]).astype(BF16)
    for b in range(4):
        near[b] = mix[:, b * LANE : (b + 1) * LANE]
        far[b] = mix[:, (b + 4) * LANE : (b + 5) * LANE]


def down(nt, info, meta, w, wrow, pt, bufs, after):
    r = nt * TILE
    return call(
        functools.partial(down_kernel, nt),
        (info, meta, w, wrow, pt, *bufs),
        [SM, SM, VM, VM, VM] + [ANY] * 5,
        (sds((4, FEAT, LANE), BF16), sds((4, FEAT, LANE), BF16), sds((r, HID), BF16)),
        (VM, VM, VM),
        [pltpu.VMEM((FEAT, r), BF16), pltpu.SemaphoreType.DMA((16,))],
        after,
    )


def dgrad_kernel(r, meta, ge, act, dgrad, tail):
    off = pl.multiple_of(meta[0] * TILE, TILE)
    for n in range(HID // 512):
        cols = slice(n * 512, (n + 1) * 512)
        tail[:r, :] = act[:, cols]
        if r < PAD:
            tail[r:, :] = jnp.zeros((PAD - r, 512), BF16)
        dgrad[0, :, cols] = dot(ge[0], tail[:SPAN, :]).astype(BF16)
        dgrad[1, :, cols] = dot(ge[1], tail[pl.ds(off, SPAN), :]).astype(BF16)


def down_grads(r, meta, ge, act, after):
    return call(
        functools.partial(dgrad_kernel, r),
        (meta, ge, act),
        [SM, VM, VM],
        (sds((2, FEAT, HID), BF16),),
        (VM,),
        [pltpu.VMEM((PAD, 512), BF16)],
        after,
    )


def line_blocks(bufs, d):
    if d == 2:
        return [(bufs[j // 2], j % 2, ARRIVE[j]) for j in range(4)]
    return [(bufs[0], j, ARRIVE[j]) for j in range(4)]


def wgrad_kernel(r, d, n_buf, fresh, info, meta, xe, *refs):
    blocks = line_blocks(refs[:n_buf], d)
    refs = refs[n_buf:] if fresh else refs[n_buf + 2 :]
    outs, (land, stage, in_sems, out_sems) = refs[:2], refs[2:]
    off = pl.multiple_of(meta[0] * TILE, TILE)
    fetch = [
        [
            pltpu.make_async_copy(
                ref.at[at, pl.ds(a * r, r), :],
                land.at[a, pl.ds(0, r), pl.ds(j * LANE, LANE)],
                in_sems.at[a * 4 + j],
            )
            for j, (ref, at, _) in enumerate(blocks)
        ]
        for a in range(2)
    ]
    store = [
        [
            pltpu.make_async_copy(
                stage.at[a, :, :, pl.ds(j * LANE, LANE)],
                outs[a].at[:, :, lanes(block_at(info, inner, d))],
                out_sems.at[a * 4 + j],
            )
            for j, (_, _, inner) in enumerate(blocks)
        ]
        for a in range(2)
    ]
    for cps in fetch:
        for cp in cps:
            cp.start()
    if r < PAD:
        land[:, r:, :] = jnp.zeros((2, PAD - r, 512), BF16)
    for a in range(2):
        for cp in fetch[a]:
            cp.wait()
        stage[a, 0] = dot(xe[0], land[a, :SPAN, :]).astype(BF16)
        stage[a, 1] = dot(xe[1], land[a, pl.ds(off, SPAN), :]).astype(BF16)
        for cp in store[a]:
            cp.start()
    for cps in store:
        for cp in cps:
            cp.wait()


def wgrad(r, d, info, meta, xe, bufs, prev, after):
    shape = sds((2, FEAT, HID), BF16)
    args = [info, meta, xe, *bufs]
    alias = {}
    if prev is not None:
        alias = {len(args): 0, len(args) + 1: 1}
        args += list(prev)
    return call(
        functools.partial(wgrad_kernel, r, d, len(bufs), prev is None),
        args,
        [SM, SM, VM] + [ANY] * (len(args) - 3),
        (shape, shape),
        (ANY, ANY),
        [
            pltpu.VMEM((2, PAD, 512), BF16),
            pltpu.VMEM((2, 2, FEAT, 512), BF16),
            pltpu.SemaphoreType.DMA((8,)),
            pltpu.SemaphoreType.DMA((8,)),
        ],
        after,
        alias=alias,
    )


def back_kernel(nt, d, n_buf, first, last, info, meta, *refs):
    r = nt * TILE
    refs = list(refs)
    prev = None if first else (refs.pop(0), refs.pop(0))
    pt = refs.pop(0) if last else None
    blocks = line_blocks(refs[:n_buf], d)
    ws = refs[n_buf : n_buf + 2]
    outs, (land, wl, tails, sems, w_sems, t_sems) = refs[n_buf + 2 : n_buf + 4], refs[-6:]
    acc, inner = refs[n_buf + 4 : n_buf + 6] if last else outs
    tiles0 = meta[0]
    fetch = [
        [
            pltpu.make_async_copy(
                ref.at[at, pl.ds(a * r, r), :], land.at[a, :, pl.ds(j * LANE, LANE)], sems.at[a * 4 + j]
            )
            for j, (ref, at, _) in enumerate(blocks)
        ]
        + [
            pltpu.make_async_copy(
                ws[a].at[:, :, lanes(block_at(info, in_, d))],
                wl.at[a, :, :, pl.ds(j * LANE, LANE)],
                w_sems.at[a * 4 + j],
            )
            for j, (_, _, in_) in enumerate(blocks)
        ]
        for a in range(2)
    ]
    sums = [
        pltpu.make_async_copy(ref.at[at, pl.ds(2 * r, 32), :], tails.at[j], t_sems.at[j])
        for j, (ref, at, _) in enumerate(blocks)
    ]
    for cp in fetch[0] + fetch[1] + sums:
        cp.start()
    for cp in sums:
        cp.wait()
    s_now = jnp.zeros((16, LANE), F32) if first else prev[1][...]
    for j in range(4):
        s_now = s_now + (tails[j, :16, :].astype(F32) + tails[j, 16:, :].astype(F32))
    inner[...] = s_now
    for a in range(2):
        for cp in fetch[a]:
            cp.wait()

    def step(i, carry):
        rows = pl.ds(pl.multiple_of(i * TILE, TILE), TILE)
        e = (i >= tiles0).astype(jnp.int32)
        now = dot_t(wl[0, e], land[0, rows, :]) + dot_t(wl[1, e], land[1, rows, :])
        acc[:, rows] = now if first else prev[0][:, rows] + now
        return carry

    lax.fori_loop(0, nt, step, 0, unroll=nt == 5)
    if last:
        near, far = outs
        total = dot(acc[...].astype(BF16), pt[...]).astype(BF16)
        s3 = jnp.concatenate(split3(s_now), axis=0)
        wide = jnp.concatenate([s3] * (r // LANE), axis=1)
        at_row = lax.broadcasted_iota(jnp.int32, (48, r), 0)
        at_row = at_row - (at_row // 16) * 16
        keep = at_row == lax.broadcasted_iota(jnp.int32, (48, r), 1) // LANE
        got = dot(jnp.where(keep, wide, jnp.zeros_like(wide)), pt[...])
        got = (got[:16] + got[16:32]) + got[32:]
        second = lax.broadcasted_iota(jnp.int32, (16, TOKS), 0) >= 2 * tiles0
        dense0 = jnp.sum(jnp.where(second, 0.0, got), axis=0, keepdims=True)
        dense1 = jnp.sum(jnp.where(second, got, 0.0), axis=0, keepdims=True)
        expert = lax.broadcasted_iota(jnp.int32, (16, TOKS), 0)
        at = info[1] * 2
        table = jnp.where(expert == at, dense0, 0.0) + jnp.where(expert == at + 1, dense1, 0.0)
        t3 = split3(table)
        for b in range(8):
            cols = slice(b * LANE, (b + 1) * LANE)
            out = (near if b < 4 else far).at[b % 4]
            out[:FEAT, :] = total[:, cols]
            for q in range(3):
                out[FEAT + 16 * q : FEAT + 16 * (q + 1), :] = t3[q][:, cols]


def back(nt, d, info, meta, bufs, wg, wu, prev, pt, after):
    r = nt * TILE
    first, last = prev is None, pt is not None
    args = [info, meta]
    specs = [SM, SM]
    if not first:
        args += list(prev)
        specs += [VM, VM]
    if last:
        args.append(pt)
        specs.append(VM)
    args += [*bufs, wg, wu]
    specs += [ANY] * (len(bufs) + 2)
    keep = [((FEAT, r), F32), ((16, LANE), F32)]
    scratch = [
        pltpu.VMEM((2, r, 512), BF16),
        pltpu.VMEM((2, 2, FEAT, 512), BF16),
        pltpu.VMEM((4, 32, LANE), BF16),
        pltpu.SemaphoreType.DMA((8,)),
        pltpu.SemaphoreType.DMA((8,)),
        pltpu.SemaphoreType.DMA((4,)),
    ]
    if last:
        out_shape = (sds((4, FEAT + 48, LANE), BF16),) * 2
        scratch = [pltpu.VMEM(*k) for k in keep] + scratch
    else:
        out_shape = tuple(sds(*k) for k in keep)
    return call(
        functools.partial(back_kernel, nt, d, len(bufs), first, last),
        args,
        specs,
        out_shape,
        (VM, VM),
        scratch,
        after,
    )


def home_kernel(own, other, ids, tg, wg):
    total = own[...].astype(F32)
    for j in range(3):
        total = total + other[j][...].astype(F32)
    tg[...] = total[:FEAT].astype(BF16)
    dense = (total[FEAT : FEAT + 16] + total[FEAT + 16 : FEAT + 32]) + total[FEAT + 32 :]
    expert = lax.broadcasted_iota(jnp.int32, (16, LANE), 0)
    for k in range(8):
        wg[k : k + 1, :] = jnp.sum(jnp.where(expert == ids[k : k + 1, :], dense, 0.0), axis=0, keepdims=True)


def home(own, a, b, c, ids):
    def kern(own, a, b, c, ids, tg, wg):
        home_kernel(own, (a, b, c), ids, tg, wg)

    return pl.pallas_call(
        kern,
        out_shape=(sds((FEAT, LANE), BF16), sds((8, LANE), F32)),
        in_specs=[VM] * 5,
        out_specs=(VM, VM),
    )(own, a, b, c, ids)


def to_experts(v):
    return [v] + [z_shift(v, -k) for k in (1, 2, 3)]


def first_stack_kernel(a, b, c, d, og, out, og_out):
    for j, v in enumerate((a, b, c, d)):
        out[j] = v[...]
    og_out[...] = og[...]


def near_kernel(near, there, *outs):
    for j in range(4):
        outs[j][...] = plus(near[j], there[j])


def to_home(near, far, after):
    there = mate(far)
    mine, tok = call(near_kernel, (near, there), [VM, VM], (sds(near.shape[1:], BF16),) * 4, (VM,) * 4, after=after)
    return [mine[0]] + [z_shift(mine[k], k) for k in (1, 2, 3)], tok


def mixed_kernel(a, b, c, d, out):
    out[...] = ((a[...].astype(F32) + b[...].astype(F32)) + (c[...].astype(F32) + d[...].astype(F32))).astype(BF16)


def both(to_right, to_left, phase):
    return hop(to_right, phase, 1), hop(to_left, phase, -1)


def passes(nt, info, ids, packed, og, w_gate, w_up, w_down):
    r = nt * TILE
    (mine, og), tok = call(
        first_stack_kernel,
        (*to_experts(packed), og),
        [VM] * 5,
        (sds((4, FEAT + 48, LANE), BF16), sds((FEAT, LANE), BF16)),
        (VM, VM),
    )
    other = mate(mine)
    og_line = to_experts(og)
    (xr, pt, wcol, wrow, meta), tok = make_rows(nt, info, mine, other, (tok,))
    gu, dn = (w_gate, w_up), (w_down,)
    og_mine, tok = stack(og_line, (tok,))
    (g1, g2), tok = parts(nt, (2,), True, info, meta, xr, gu, (tok,))
    g_in = both(g1, g2, 0)
    og_other = mate(og_mine)
    (gr, xe, ge), tok = make_grads(nt, meta, og_mine, og_other, xr, pt, wcol, (tok,))
    (a1, a2), tok = parts(nt, (2,), True, info, meta, gr, dn, (tok,))
    a_in = both(a1, a2, 0)
    (g_rt, g_lf), tok = parts(nt, (1, -1), False, info, meta, xr, gu, (tok,))
    (g_rt, g_lf), tok = join(g_rt, g_lf, *g_in, (tok,))
    (g_rt, g_lf), tok = gate((g_rt, g_lf), (tok, *a_in))
    g_in = both(g_rt, g_lf, 0)
    (a_rt, a_lf), tok = parts(nt, (1, -1), False, info, meta, gr, dn, (tok,))
    (a_rt, a_lf), tok = join(a_rt, a_lf, *a_in, (tok,))
    a_in = both(a_rt, a_lf, 0)
    (g_own,), tok = parts(nt, (0,), False, info, meta, xr, gu, (tok,))
    (a_own,), tok = parts(nt, (0,), False, info, meta, gr, dn, (tok,))
    (h1, h2, g_rt, g_lf, g_own), tok = turn(g_own, *g_in, (tok,))
    g_in = both(h1, h2, 1)
    (g_rt, g_lf), tok = join_rows(g_rt, g_lf, *g_in, (tok,))
    g_in = both(g_rt, g_lf, 1)
    (h1, h2, a_rt, a_lf, a_own), tok = turn(a_own, *a_in, (tok,))
    a_in = both(h1, h2, 1)
    (gates, ups, act), tok = make_act(r, (g_own, *g_in), (tok,))
    c_in = both(act, act, 0)
    (a_rt, a_lf), tok = join_rows(a_rt, a_lf, *a_in, (tok,))
    a_in = both(a_rt, a_lf, 1)
    (h1, h2), tok = halves(*c_in, (tok,))
    c_far = both(h1, h2, 0)
    delta, tok = make_deltas(r, (gates, ups, wcol, a_own, *a_in), (tok,))
    d_in = both(delta, delta, 0)
    c_line, tok = line(act, c_in[1], c_in[0], *c_far, (tok,))
    c_left, c_right = both(c_line, c_line, 1)
    (h1, h2), tok = halves(*d_in, (tok,))
    d_far = both(h1, h2, 0)
    (h1, h2), tok = halves(c_left, c_right, (tok,))
    c_far = both(h1, h2, 1)
    d_line, tok = line(delta, d_in[1], d_in[0], *d_far, (tok, *c_far))
    d_left, d_right = both(d_line, d_line, 1)

    def back_of(d, bufs, acc, table):
        return back(nt, d, info, meta, bufs, w_gate, w_up, acc, table, (tok,))

    def wgrad_of(d, bufs, prev):
        return wgrad(r, d, info, meta, xe, bufs, prev, (tok,))

    (near, far, act_all), tok = down(nt, info, meta, w_down, wrow, pt, (c_line, c_right, c_left, *c_far), (tok,))
    acc, tok = back_of(0, (d_line,), None, None)
    grads, tok = wgrad_of(0, (d_line,), None)
    mixed_home, tok = to_home(near, far, (tok,))
    (down_grad,), tok = down_grads(r, meta, ge, act_all, (tok,))
    (h1, h2), tok = halves(d_left, d_right, (tok,))
    d_far = both(h1, h2, 1)
    acc, tok = back_of(1, (d_right,), acc, None)
    acc, tok = back_of(-1, (d_left,), acc, None)
    grads, tok = wgrad_of(1, (d_right,), grads)
    grads, tok = wgrad_of(-1, (d_left,), grads)
    (mixed,), tok = call(mixed_kernel, mixed_home, [VM] * 4, (sds((FEAT, LANE), BF16),), (VM,), after=(tok,))
    (near, far), tok = back_of(2, d_far, acc, pt)
    token_home, _ = to_home(near, far, ())
    (gate_grad, up_grad), tok = wgrad_of(2, d_far, grads)
    token_grad, weight_grad = home(*token_home, ids)
    return meta[2], (mixed, token_grad, weight_grad, gate_grad, up_grad, down_grad)


def body(tokens, expert_ids, route_weights, output_grad, w_gate, w_up, w_down):
    info = jnp.stack([lax.axis_index("ctx"), lax.axis_index("exp")]).astype(jnp.int32)
    ids = expert_ids.T
    og = output_grad.T
    weights = (w_gate, w_up, w_down.transpose(0, 2, 1))
    packed = pack(tokens.T, ids, route_weights.T)
    most, outs = passes(5, info, ids, packed, og, *weights)

    def again(state):
        return jnp.zeros_like(state[0]), passes(6, info, ids, packed, og, *weights)[1]

    _, outs = lax.while_loop(lambda state: state[0] > 5, again, (most, outs))
    mixed, token_grad, weight_grad, gate_grad, up_grad, down_grad = outs
    return (
        mixed.T,
        token_grad.T,
        weight_grad.T,
        gate_grad,
        up_grad,
        down_grad.transpose(0, 2, 1),
    )


def solution(mesh):
    return jax.shard_map(
        body,
        mesh=mesh,
        in_specs=(
            P("exp", "ctx"),
            P("exp", None),
            P("exp", None),
            P("exp", "ctx"),
            P("exp", "ctx", None),
            P("exp", "ctx", None),
            P("exp", None, "ctx"),
        ),
        out_specs=(
            P("exp", "ctx"),
            P("exp", "ctx"),
            P("exp", None),
            P("exp", "ctx", None),
            P("exp", "ctx", None),
            P("exp", None, "ctx"),
        ),
        check_vma=False,
    )
```

```python
import functools

import jax
import jax.numpy as jnp
from jax import lax
from jax.experimental import pallas as pl
from jax.experimental.pallas import tpu as pltpu
from jax.sharding import PartitionSpec as P

F32 = jnp.float32
BF16 = jnp.bfloat16
TILE = 256
LANE = 128
FEAT = 448
HID = 2048
SPAN = 768
PAD = 2 * SPAN
LEAVE = (2, 1, -1, 0)
ARRIVE = (0, 1, -1, 2)
TOKS = 1024
BOTH = ("ctx", "exp")
VM = pl.BlockSpec(memory_space=pltpu.VMEM)
SM = pl.BlockSpec(memory_space=pltpu.SMEM)
ANY = pl.BlockSpec(memory_space=pl.ANY)


def params(mib):
    return pltpu.CompilerParams(vmem_limit_bytes=mib * 1024 * 1024)


def sds(shape, dtype):
    return jax.ShapeDtypeStruct(shape, dtype)


def call(kern, args, specs, out_shape, out_specs, scratch=(), after=(), mib=32, alias=None):
    n_in, n_out = len(args), len(out_shape)
    skip = n_in + len(after)

    def wrapped(*refs):
        kern(*refs[:n_in], *refs[skip : skip + n_out], *refs[skip + n_out + 1 :])

    res = pl.pallas_call(
        wrapped,
        out_shape=(*out_shape, sds((8, LANE), F32)),
        in_specs=[*specs] + [ANY] * len(after),
        out_specs=(*out_specs, ANY),
        scratch_shapes=list(scratch),
        input_output_aliases=alias or {},
        compiler_params=params(mib),
        cost_estimate=pl.CostEstimate(flops=1, bytes_accessed=1, transcendentals=0),
    )(*args, *after)
    return res[:-1], res[-1]


def dot(a, b):
    return lax.dot_general(a, b, (((1,), (0,)), ((), ())), preferred_element_type=F32)


def dot_t(a, b):
    return lax.dot_general(a, b, (((1,), (1,)), ((), ())), preferred_element_type=F32)


def hop(v, phase, step):
    pairs = []
    for y in range(4):
        for x in range(4):
            for e in range(8):
                along_x = (e % 2 == 0) == (phase == 0)
                to = (y * 4 + (x + step) % 4) if along_x else (((y + step) % 4) * 4 + x)
                pairs.append(((y * 4 + x) * 8 + e, to * 8 + e))
    return lax.ppermute(v, BOTH, pairs)


def z_shift(v, k):
    return lax.ppermute(v, "exp", [(z * 2 + c, ((z + k) % 4) * 2 + c) for z in range(4) for c in range(2)])


def mate(v):
    return lax.ppermute(v, "exp", [(e, e ^ 1) for e in range(8)])


def block_at(info, d0, d1):
    ctx = info[0]
    y = ctx // 4
    x = ctx - y * 4
    odd = info[1] - (info[1] // 2) * 2
    dx = d0 + odd * (d1 - d0)
    dy = d1 + odd * (d0 - d1)
    return jnp.bitwise_and(y + dy + 8, 3) * 4 + jnp.bitwise_and(x + dx + 8, 3)


def lanes(c):
    return pl.ds(pl.multiple_of(c * LANE, LANE), LANE)


def pack_kernel(tok, ids, rw, out):
    out[:FEAT, :] = tok[...]
    expert = lax.broadcasted_iota(jnp.int32, (16, LANE), 0)
    dense = jnp.zeros((16, LANE), F32)
    for k in range(8):
        dense += jnp.where(ids[k : k + 1, :] == expert, rw[k : k + 1, :], 0.0)
    for i, part in enumerate(split3(dense)):
        out[FEAT + 16 * i : FEAT + 16 * (i + 1), :] = part


def split3(v):
    hi = v.astype(BF16)
    rest = v - hi.astype(F32)
    mid = rest.astype(BF16)
    low = (rest - mid.astype(F32)).astype(BF16)
    return hi, mid, low


def pack(tok, ids, rw):
    return pl.pallas_call(pack_kernel, out_shape=sds((FEAT + 48, LANE), BF16), in_specs=[VM] * 3, out_specs=VM)(
        tok, ids, rw
    )


def rows_kernel(nt, info, mine, other, xr, pt, wcol, wrow, meta, tt_out):
    blocks = [mine[j] for j in range(4)] + [other[j] for j in range(4)]
    tt = jnp.concatenate([b[:FEAT, :] for b in blocks], axis=1)
    expert = lax.broadcasted_iota(jnp.int32, (16, LANE), 0)
    first = info[1] * 2
    weights = [[], []]
    named = jnp.zeros((16, 1), F32)
    for b in blocks:
        tail = b[FEAT : FEAT + 48, :].astype(F32)
        dense = (tail[:16] + tail[16:32]) + tail[32:48]
        named += jnp.sum((dense > 0.0).astype(F32), axis=1, keepdims=True)
        for l in range(2):
            weights[l].append(jnp.sum(jnp.where(expert == first + l, dense, 0.0), axis=0, keepdims=True))
    member = [[(w > 0.0).astype(F32) for w in ws] for ws in weights]
    before = (
        lax.broadcasted_iota(jnp.int32, (LANE, LANE), 0) < lax.broadcasted_iota(jnp.int32, (LANE, LANE), 1)
    ).astype(BF16)
    ranks = dot(jnp.concatenate(member[0] + member[1], axis=0).astype(BF16), before)
    slots = []
    base = jnp.zeros((1, 1), F32)
    for l in range(2):
        run = base
        for b in range(8):
            m = member[l][b]
            slots.append(jnp.where(m > 0.0, ranks[l * 8 + b : l * 8 + b + 1, :] + run, -1.0))
            run = run + jnp.sum(m, axis=1, keepdims=True)
        if l == 0:
            base = jnp.maximum(jnp.floor((run + (TILE - 1.0)) * (1.0 / TILE)), 1.0) * TILE
    count = jnp.sum(jnp.concatenate(member[0], axis=0)).astype(jnp.int32)
    meta[0] = jnp.maximum((count + (TILE - 1)) // TILE, 1)
    count = jnp.sum(jnp.concatenate(member[1], axis=0)).astype(jnp.int32)
    meta[1] = jnp.maximum((count + (TILE - 1)) // TILE, 1)
    tiles = jnp.broadcast_to(jnp.maximum(jnp.floor((named + (TILE - 1.0)) * (1.0 / TILE)), 1.0), (16, LANE))
    even = lax.broadcasted_iota(jnp.int32, (16, 16), 0) // 2 == lax.broadcasted_iota(jnp.int32, (16, 16), 1) // 2
    most = jnp.max(dot(even.astype(BF16), tiles.astype(BF16))).astype(jnp.int32)
    meta[2] = most
    tt_out[...] = tt
    q0 = jnp.concatenate(slots[:8], axis=1).astype(jnp.int32)
    q1 = jnp.concatenate(slots[8:], axis=1).astype(jnp.int32)
    w0 = jnp.concatenate(weights[0], axis=1)
    w1 = jnp.concatenate(weights[1], axis=1)

    def tile_rows(i, carry):
        sl = pl.ds(pl.multiple_of(i * TILE, TILE), TILE)
        row = lax.broadcasted_iota(jnp.int32, (TILE, TOKS), 0) + i * TILE
        hit0, hit1 = row == q0, row == q1
        one = jnp.where(hit0 | hit1, 1.0, 0.0).astype(BF16)
        pt[sl, :] = one
        col = jnp.sum(jnp.where(hit0, w0, 0.0) + jnp.where(hit1, w1, 0.0), axis=1, keepdims=True)
        wide = jnp.broadcast_to(col, (TILE, LANE))
        wcol[sl, :] = wide
        wrow[:, sl] = jnp.transpose(wide)[:8, :]
        xr[sl, :] = dot_t(one, tt_out[...]).astype(BF16)
        return carry

    lax.fori_loop(0, nt, tile_rows, 0)


def make_rows(nt, info, mine, other, after):
    r = nt * TILE
    return call(
        functools.partial(rows_kernel, nt),
        (info, mine, other),
        [SM, VM, VM],
        (
            sds((r, FEAT), BF16),
            sds((r, TOKS), BF16),
            sds((r, LANE), F32),
            sds((8, r), F32),
            sds((8,), jnp.int32),
        ),
        (VM, VM, VM, VM, SM),
        [pltpu.VMEM((FEAT, TOKS), BF16)],
        after,
    )


def grads_kernel(nt, meta, mine, other, xr, pt, wcol, gr, xe, ge, gg, turned):
    r = nt * TILE
    off = pl.multiple_of(meta[0] * TILE, TILE)
    for j in range(4):
        gg[:, j * LANE : (j + 1) * LANE] = mine[j]
        gg[:, (j + 4) * LANE : (j + 5) * LANE] = other[j]
    if r < PAD:
        turned[:, :, r:] = jnp.zeros((2, FEAT, PAD - r), BF16)

    def tile_step(i, carry):
        sl = pl.ds(pl.multiple_of(i * TILE, TILE), TILE)
        g = (dot_t(pt[sl, :], gg[...]) * wcol[sl, :1]).astype(BF16)
        gr[sl, :] = g
        turned[0, :, sl] = jnp.transpose(xr[sl, :])
        turned[1, :, sl] = jnp.transpose(g)
        return carry

    lax.fori_loop(0, nt, tile_step, 0, unroll=nt == 5)
    mine_too = lax.broadcasted_iota(jnp.int32, (FEAT, SPAN), 1) < off
    zero = jnp.zeros((FEAT, SPAN), BF16)
    for q, out in ((0, xe), (1, ge)):
        out[0] = jnp.where(mine_too, turned[q, :, :SPAN], zero)
        out[1] = turned[q, :, pl.ds(off, SPAN)]


def make_grads(nt, meta, mine, other, xr, pt, wcol, after):
    r = nt * TILE
    span = sds((2, FEAT, SPAN), BF16)
    return call(
        functools.partial(grads_kernel, nt),
        (meta, mine, other, xr, pt, wcol),
        [SM] + [VM] * 5,
        (sds((r, FEAT), BF16), span, span),
        (VM, VM, VM),
        [pltpu.VMEM((FEAT, TOKS), BF16), pltpu.VMEM((2, FEAT, PAD), BF16)],
        after,
    )


def parts_kernel(nt, outers, split, n_w, info, meta, src, *refs):
    weights, refs = refs[:n_w], refs[n_w:]
    n_out = len(outers) * (2 if split else 1)
    outs, (bufs, sems) = refs[:n_out], refs[n_out:]
    jobs = [(p, w) for p in range(len(outers)) for w in range(n_w)]
    copies = [
        [
            pltpu.make_async_copy(
                weights[w].at[:, :, lanes(block_at(info, outers[p], LEAVE[i]))],
                bufs.at[n, :, :, pl.ds(i * LANE, LANE)],
                sems.at[n * 4 + i],
            )
            for i in range(4)
        ]
        for n, (p, w) in enumerate(jobs)
    ]
    for cps in copies:
        for cp in cps:
            cp.start()
    tiles0 = meta[0]
    for n, (p, w) in enumerate(jobs):
        for cp in copies[n]:
            cp.wait()

        def tile_step(t, carry, n=n, p=p, w=w):
            sl = pl.ds(pl.multiple_of(t * TILE, TILE), TILE)
            e = (t >= tiles0).astype(jnp.int32)
            out = dot(src[sl, :], bufs[n, e]).astype(BF16)
            for i in range(4):
                o, at = (outs[2 * p + i // 2], i % 2) if split else (outs[p], i)
                o[at, w, sl, :] = out[:, i * LANE : (i + 1) * LANE]
            return carry

        lax.fori_loop(0, nt, tile_step, 0, unroll=nt == 5)


def parts(nt, outers, split, info, meta, src, weights, after):
    n_w = len(weights)
    shape = sds((2 if split else 4, n_w, nt * TILE, LANE), BF16)
    n_out = len(outers) * (2 if split else 1)
    return call(
        functools.partial(parts_kernel, nt, outers, split, n_w),
        (info, meta, src, *weights),
        [SM, SM, VM] + [ANY] * n_w,
        (shape,) * n_out,
        (VM,) * n_out,
        [
            pltpu.VMEM((len(outers) * n_w, 2, FEAT, 512), BF16),
            pltpu.SemaphoreType.DMA((4 * len(outers) * n_w,)),
        ],
        after,
    )


def tiles_of(n, size, body):
    def step(i, carry):
        body(pl.ds(pl.multiple_of(i * size, size), size))
        return carry

    lax.fori_loop(0, n // size, step, 0)


def plus(a, b):
    return (a.astype(F32) + b.astype(F32)).astype(BF16)


def join_kernel(n_w, r, rt, lf, from_left, from_right, rt_out, lf_out):
    for w in range(n_w):

        def rows(sl, w=w):
            for i in range(2):
                rt_out[i, w, sl, :] = plus(rt[i, w, sl, :], from_left[i, w, sl, :])
                rt_out[i + 2, w, sl, :] = rt[i + 2, w, sl, :]
                lf_out[i, w, sl, :] = lf[i, w, sl, :]
                lf_out[i + 2, w, sl, :] = plus(lf[i + 2, w, sl, :], from_right[i, w, sl, :])

        tiles_of(r, TILE, rows)


def join(rt, lf, from_left, from_right, after):
    return call(
        functools.partial(join_kernel, rt.shape[1], rt.shape[2]),
        (rt, lf, from_left, from_right),
        [VM] * 4,
        (sds(rt.shape, BF16),) * 2,
        (VM, VM),
        after=after,
    )


def gate(vs, after):
    return call(
        lambda *refs: None,
        vs,
        [ANY] * len(vs),
        tuple(sds(v.shape, v.dtype) for v in vs),
        (ANY,) * len(vs),
        after=after,
        alias={i: i for i in range(len(vs))},
    )


def turn_kernel(n_w, r, own, from_left, from_right, h1, h2, rt, lf, rest):
    half = r // 2

    def total(i, w, sl):
        return (
            own[i, w, sl, :].astype(F32) + from_left[i, w, sl, :].astype(F32) + from_right[i, w, sl, :].astype(F32)
        ).astype(BF16)

    for w in range(n_w):

        def rows(sl, w=w):
            h1[w, sl, :] = total(0, w, sl)
            h2[w, sl, :] = total(0, w, pl.ds(pl.multiple_of(sl.start + half, LANE), LANE))

        tiles_of(half, LANE, rows)

        def others(sl, w=w):
            for i, out in ((1, rt), (2, lf), (3, rest)):
                out[w, sl, :] = total(i, w, sl)

        tiles_of(r, TILE, others)


def turn(own, from_left, from_right, after):
    _, n_w, r, _ = own.shape
    half, full = sds((n_w, r // 2, LANE), BF16), sds((n_w, r, LANE), BF16)
    return call(
        functools.partial(turn_kernel, n_w, r),
        (own, from_left, from_right),
        [VM] * 3,
        (half, half, full, full, full),
        (VM,) * 5,
        after=after,
    )


def join_rows_kernel(n_w, r, rt, lf, from_left, from_right, rt_out, lf_out):
    half = r // 2
    for w in range(n_w):

        def rows(sl, w=w):
            up = pl.ds(pl.multiple_of(sl.start + half, LANE), LANE)
            rt_out[w, sl, :] = plus(rt[w, sl, :], from_left[w, sl, :])
            rt_out[w, up, :] = rt[w, up, :]
            lf_out[w, sl, :] = lf[w, sl, :]
            lf_out[w, up, :] = plus(lf[w, up, :], from_right[w, sl, :])

        tiles_of(half, LANE, rows)


def join_rows(rt, lf, from_left, from_right, after):
    return call(
        functools.partial(join_rows_kernel, rt.shape[0], rt.shape[1]),
        (rt, lf, from_left, from_right),
        [VM] * 4,
        (sds(rt.shape, BF16),) * 2,
        (VM, VM),
        after=after,
    )


def total3(refs, w, sl):
    return refs[0][w, sl, :].astype(F32) + refs[1][w, sl, :].astype(F32) + refs[2][w, sl, :].astype(F32)


def act_kernel(r, a, b, c, gates, ups, act):
    def rows(sl):
        gate = total3((a, b, c), 0, sl)
        up = total3((a, b, c), 1, sl)
        gates[sl, :] = gate
        ups[sl, :] = up
        act[sl, :] = (gate / (1.0 + jnp.exp(-gate)) * up).astype(BF16)

    tiles_of(r, LANE, rows)


def make_act(r, args, after):
    full = sds((r, LANE), F32)
    return call(
        functools.partial(act_kernel, r),
        args,
        [VM] * 3,
        (full, full, sds((r, LANE), BF16)),
        (VM,) * 3,
        after=after,
    )


def delta_kernel(r, gates, ups, wcol, a, b, c, out, sums):
    sums[...] = jnp.zeros_like(sums)

    def step(i, carry):
        sl = pl.ds(pl.multiple_of(i * LANE, LANE), LANE)
        gate = gates[sl, :]
        up = ups[sl, :]
        ag = total3((a, b, c), 0, sl)
        s = 1.0 / (1.0 + jnp.exp(-gate))
        silu = gate * s
        out[sl, :] = (ag * up * s * (1.0 + gate * (1.0 - s))).astype(BF16)
        out[pl.ds(pl.multiple_of(r + i * LANE, LANE), LANE), :] = (ag * silu).astype(BF16)
        act = (gate / (1.0 + jnp.exp(-gate)) * up).astype(BF16).astype(F32)
        w = wcol[sl, :]
        inner = act * ag * jnp.where(w > 0.0, 1.0 / jnp.maximum(w, 1e-6), 0.0)
        sums[pl.ds(i, 1), :] = jnp.sum(jnp.transpose(inner), axis=0, keepdims=True)
        return carry

    lax.fori_loop(0, r // LANE, step, 0)
    total = sums[...]
    hi = total.astype(BF16)
    out[2 * r : 2 * r + 16, :] = hi
    out[2 * r + 16 :, :] = (total - hi.astype(F32)).astype(BF16)


def make_deltas(r, args, after):
    (out,), tok = call(
        functools.partial(delta_kernel, r),
        args,
        [VM] * 6,
        (sds((2 * r + 32, LANE), BF16),),
        (VM,),
        [pltpu.VMEM((16, LANE), F32)],
        after,
    )
    return out, tok


def halves_kernel(n, from_left, from_right, h1, h2):
    h1[...] = from_left[:n]
    h2[...] = from_right[n:]


def halves(from_left, from_right, after):
    n = from_left.shape[0] // 2
    shape = sds((n, *from_left.shape[1:]), BF16)
    return call(
        functools.partial(halves_kernel, n), (from_left, from_right), [VM] * 2, (shape, shape), (VM, VM), after=after
    )


def line_kernel(n, own, from_right, from_left, o1, o2, out):
    out[0] = own[...]
    out[1] = from_right[...]
    out[2] = from_left[...]
    out[3, :n, :] = o1[...]
    out[3, n:, :] = o2[...]


def line(own, from_right, from_left, o1, o2, after):
    (out,), tok = call(
        functools.partial(line_kernel, o1.shape[0]),
        (own, from_right, from_left, o1, o2),
        [VM] * 5,
        (sds((4, *own.shape), BF16),),
        (VM,),
        after=after,
    )
    return out, tok


def stack_kernel(a, b, c, d, out):
    for j, v in enumerate((a, b, c, d)):
        out[j] = v[...]


def stack(vs, after):
    (out,), tok = call(stack_kernel, vs, [VM] * 4, (sds((4, *vs[0].shape), BF16),), (VM,), after=after)
    return out, tok


def down_kernel(nt, info, meta, w, wrow, pt, b0, br, bl, o1, o2, near, far, act, y, sems):
    r = nt * TILE
    copies = []
    for d, refs in ((0, (b0, b0, b0, b0)), (1, (br,) * 4), (-1, (bl,) * 4), (2, (o1, o1, o2, o2))):
        for j in range(4):
            at = j % 2 if d == 2 else j
            copies.append(
                pltpu.make_async_copy(
                    refs[j].at[at], act.at[:, lanes(block_at(info, d, ARRIVE[j]))], sems.at[len(copies)]
                )
            )
    for cp in copies:
        cp.start()
    for cp in copies:
        cp.wait()
    tiles0 = meta[0]

    def tile_step(i, carry):
        rows = pl.ds(pl.multiple_of(i * TILE, TILE), TILE)
        e = (i >= tiles0).astype(jnp.int32)
        y[:, rows] = (dot_t(w[e], act[rows, :]) * wrow[:1, rows]).astype(BF16)
        return carry

    lax.fori_loop(0, nt, tile_step, 0)
    mix = dot(y[...], pt[...]).astype(BF16)
    for b in range(4):
        near[b] = mix[:, b * LANE : (b + 1) * LANE]
        far[b] = mix[:, (b + 4) * LANE : (b + 5) * LANE]


def down(nt, info, meta, w, wrow, pt, bufs, after):
    r = nt * TILE
    return call(
        functools.partial(down_kernel, nt),
        (info, meta, w, wrow, pt, *bufs),
        [SM, SM, VM, VM, VM] + [ANY] * 5,
        (sds((4, FEAT, LANE), BF16), sds((4, FEAT, LANE), BF16), sds((r, HID), BF16)),
        (VM, VM, VM),
        [pltpu.VMEM((FEAT, r), BF16), pltpu.SemaphoreType.DMA((16,))],
        after,
    )


def dgrad_kernel(r, meta, ge, act, dgrad, tail):
    off = pl.multiple_of(meta[0] * TILE, TILE)
    for n in range(HID // 512):
        cols = slice(n * 512, (n + 1) * 512)
        tail[:r, :] = act[:, cols]
        if r < PAD:
            tail[r:, :] = jnp.zeros((PAD - r, 512), BF16)
        dgrad[0, :, cols] = dot(ge[0], tail[:SPAN, :]).astype(BF16)
        dgrad[1, :, cols] = dot(ge[1], tail[pl.ds(off, SPAN), :]).astype(BF16)


def down_grads(r, meta, ge, act, after):
    return call(
        functools.partial(dgrad_kernel, r),
        (meta, ge, act),
        [SM, VM, VM],
        (sds((2, FEAT, HID), BF16),),
        (VM,),
        [pltpu.VMEM((PAD, 512), BF16)],
        after,
    )


def line_blocks(bufs, d):
    if d == 2:
        return [(bufs[j // 2], j % 2, ARRIVE[j]) for j in range(4)]
    return [(bufs[0], j, ARRIVE[j]) for j in range(4)]


def wgrad_kernel(r, d, n_buf, fresh, info, meta, xe, *refs):
    blocks = line_blocks(refs[:n_buf], d)
    refs = refs[n_buf:] if fresh else refs[n_buf + 2 :]
    outs, (land, stage, in_sems, out_sems) = refs[:2], refs[2:]
    off = pl.multiple_of(meta[0] * TILE, TILE)
    fetch = [
        [
            pltpu.make_async_copy(
                ref.at[at, pl.ds(a * r, r), :],
                land.at[a, pl.ds(0, r), pl.ds(j * LANE, LANE)],
                in_sems.at[a * 4 + j],
            )
            for j, (ref, at, _) in enumerate(blocks)
        ]
        for a in range(2)
    ]
    store = [
        [
            pltpu.make_async_copy(
                stage.at[a, :, :, pl.ds(j * LANE, LANE)],
                outs[a].at[:, :, lanes(block_at(info, d, inner))],
                out_sems.at[a * 4 + j],
            )
            for j, (_, _, inner) in enumerate(blocks)
        ]
        for a in range(2)
    ]
    for cps in fetch:
        for cp in cps:
            cp.start()
    if r < PAD:
        land[:, r:, :] = jnp.zeros((2, PAD - r, 512), BF16)
    for a in range(2):
        for cp in fetch[a]:
            cp.wait()
        stage[a, 0] = dot(xe[0], land[a, :SPAN, :]).astype(BF16)
        stage[a, 1] = dot(xe[1], land[a, pl.ds(off, SPAN), :]).astype(BF16)
        for cp in store[a]:
            cp.start()
    for cps in store:
        for cp in cps:
            cp.wait()


def wgrad(r, d, info, meta, xe, bufs, prev, after):
    shape = sds((2, FEAT, HID), BF16)
    args = [info, meta, xe, *bufs]
    alias = {}
    if prev is not None:
        alias = {len(args): 0, len(args) + 1: 1}
        args += list(prev)
    return call(
        functools.partial(wgrad_kernel, r, d, len(bufs), prev is None),
        args,
        [SM, SM, VM] + [ANY] * (len(args) - 3),
        (shape, shape),
        (ANY, ANY),
        [
            pltpu.VMEM((2, PAD, 512), BF16),
            pltpu.VMEM((2, 2, FEAT, 512), BF16),
            pltpu.SemaphoreType.DMA((8,)),
            pltpu.SemaphoreType.DMA((8,)),
        ],
        after,
        alias=alias,
    )


def back_kernel(nt, d, n_buf, first, last, info, meta, *refs):
    r = nt * TILE
    refs = list(refs)
    prev = None if first else (refs.pop(0), refs.pop(0))
    pt = refs.pop(0) if last else None
    blocks = line_blocks(refs[:n_buf], d)
    ws = refs[n_buf : n_buf + 2]
    outs, (land, wl, tails, sems, w_sems, t_sems) = refs[n_buf + 2 : n_buf + 4], refs[-6:]
    acc, inner = refs[n_buf + 4 : n_buf + 6] if last else outs
    tiles0 = meta[0]
    fetch = [
        [
            pltpu.make_async_copy(
                ref.at[at, pl.ds(a * r, r), :], land.at[a, :, pl.ds(j * LANE, LANE)], sems.at[a * 4 + j]
            )
            for j, (ref, at, _) in enumerate(blocks)
        ]
        + [
            pltpu.make_async_copy(
                ws[a].at[:, :, lanes(block_at(info, d, in_))],
                wl.at[a, :, :, pl.ds(j * LANE, LANE)],
                w_sems.at[a * 4 + j],
            )
            for j, (_, _, in_) in enumerate(blocks)
        ]
        for a in range(2)
    ]
    sums = [
        pltpu.make_async_copy(ref.at[at, pl.ds(2 * r, 32), :], tails.at[j], t_sems.at[j])
        for j, (ref, at, _) in enumerate(blocks)
    ]
    for cp in fetch[0] + fetch[1] + sums:
        cp.start()
    for cp in sums:
        cp.wait()
    s_now = jnp.zeros((16, LANE), F32) if first else prev[1][...]
    for j in range(4):
        s_now = s_now + (tails[j, :16, :].astype(F32) + tails[j, 16:, :].astype(F32))
    inner[...] = s_now
    for a in range(2):
        for cp in fetch[a]:
            cp.wait()

    def step(i, carry):
        rows = pl.ds(pl.multiple_of(i * TILE, TILE), TILE)
        e = (i >= tiles0).astype(jnp.int32)
        now = dot_t(wl[0, e], land[0, rows, :]) + dot_t(wl[1, e], land[1, rows, :])
        acc[:, rows] = now if first else prev[0][:, rows] + now
        return carry

    lax.fori_loop(0, nt, step, 0, unroll=nt == 5)
    if last:
        near, far = outs
        total = dot(acc[...].astype(BF16), pt[...]).astype(BF16)
        s3 = jnp.concatenate(split3(s_now), axis=0)
        wide = jnp.concatenate([s3] * (r // LANE), axis=1)
        at_row = lax.broadcasted_iota(jnp.int32, (48, r), 0)
        at_row = at_row - (at_row // 16) * 16
        keep = at_row == lax.broadcasted_iota(jnp.int32, (48, r), 1) // LANE
        got = dot(jnp.where(keep, wide, jnp.zeros_like(wide)), pt[...])
        got = (got[:16] + got[16:32]) + got[32:]
        second = lax.broadcasted_iota(jnp.int32, (16, TOKS), 0) >= 2 * tiles0
        dense0 = jnp.sum(jnp.where(second, 0.0, got), axis=0, keepdims=True)
        dense1 = jnp.sum(jnp.where(second, got, 0.0), axis=0, keepdims=True)
        expert = lax.broadcasted_iota(jnp.int32, (16, TOKS), 0)
        at = info[1] * 2
        table = jnp.where(expert == at, dense0, 0.0) + jnp.where(expert == at + 1, dense1, 0.0)
        t3 = split3(table)
        for b in range(8):
            cols = slice(b * LANE, (b + 1) * LANE)
            out = (near if b < 4 else far).at[b % 4]
            out[:FEAT, :] = total[:, cols]
            for q in range(3):
                out[FEAT + 16 * q : FEAT + 16 * (q + 1), :] = t3[q][:, cols]


def back(nt, d, info, meta, bufs, wg, wu, prev, pt, after):
    r = nt * TILE
    first, last = prev is None, pt is not None
    args = [info, meta]
    specs = [SM, SM]
    if not first:
        args += list(prev)
        specs += [VM, VM]
    if last:
        args.append(pt)
        specs.append(VM)
    args += [*bufs, wg, wu]
    specs += [ANY] * (len(bufs) + 2)
    keep = [((FEAT, r), F32), ((16, LANE), F32)]
    scratch = [
        pltpu.VMEM((2, r, 512), BF16),
        pltpu.VMEM((2, 2, FEAT, 512), BF16),
        pltpu.VMEM((4, 32, LANE), BF16),
        pltpu.SemaphoreType.DMA((8,)),
        pltpu.SemaphoreType.DMA((8,)),
        pltpu.SemaphoreType.DMA((4,)),
    ]
    if last:
        out_shape = (sds((4, FEAT + 48, LANE), BF16),) * 2
        scratch = [pltpu.VMEM(*k) for k in keep] + scratch
    else:
        out_shape = tuple(sds(*k) for k in keep)
    return call(
        functools.partial(back_kernel, nt, d, len(bufs), first, last),
        args,
        specs,
        out_shape,
        (VM, VM),
        scratch,
        after,
    )


def home_kernel(own, other, ids, tg, wg):
    total = own[...].astype(F32)
    for j in range(3):
        total = total + other[j][...].astype(F32)
    tg[...] = total[:FEAT].astype(BF16)
    dense = (total[FEAT : FEAT + 16] + total[FEAT + 16 : FEAT + 32]) + total[FEAT + 32 :]
    expert = lax.broadcasted_iota(jnp.int32, (16, LANE), 0)
    for k in range(8):
        wg[k : k + 1, :] = jnp.sum(jnp.where(expert == ids[k : k + 1, :], dense, 0.0), axis=0, keepdims=True)


def home(own, a, b, c, ids):
    def kern(own, a, b, c, ids, tg, wg):
        home_kernel(own, (a, b, c), ids, tg, wg)

    return pl.pallas_call(
        kern,
        out_shape=(sds((FEAT, LANE), BF16), sds((8, LANE), F32)),
        in_specs=[VM] * 5,
        out_specs=(VM, VM),
    )(own, a, b, c, ids)


def to_experts(v):
    return [v] + [z_shift(v, -k) for k in (1, 2, 3)]


def first_stack_kernel(a, b, c, d, og, out, og_out):
    for j, v in enumerate((a, b, c, d)):
        out[j] = v[...]
    og_out[...] = og[...]


def near_kernel(near, there, *outs):
    for j in range(4):
        outs[j][...] = plus(near[j], there[j])


def to_home(near, far, after):
    there = mate(far)
    mine, tok = call(near_kernel, (near, there), [VM, VM], (sds(near.shape[1:], BF16),) * 4, (VM,) * 4, after=after)
    return [mine[0]] + [z_shift(mine[k], k) for k in (1, 2, 3)], tok


def mixed_kernel(a, b, c, d, out):
    out[...] = ((a[...].astype(F32) + b[...].astype(F32)) + (c[...].astype(F32) + d[...].astype(F32))).astype(BF16)


def both(to_right, to_left, phase):
    return hop(to_right, phase, 1), hop(to_left, phase, -1)


def passes(nt, info, ids, packed, og, w_gate, w_up, w_down):
    r = nt * TILE
    (mine, og), tok = call(
        first_stack_kernel,
        (*to_experts(packed), og),
        [VM] * 5,
        (sds((4, FEAT + 48, LANE), BF16), sds((FEAT, LANE), BF16)),
        (VM, VM),
    )
    other = mate(mine)
    og_line = to_experts(og)
    (xr, pt, wcol, wrow, meta), tok = make_rows(nt, info, mine, other, (tok,))
    gu, dn = (w_gate, w_up), (w_down,)
    og_mine, tok = stack(og_line, (tok,))
    (g1, g2), tok = parts(nt, (2,), True, info, meta, xr, gu, (tok,))
    g_in = both(g1, g2, 0)
    og_other = mate(og_mine)
    (gr, xe, ge), tok = make_grads(nt, meta, og_mine, og_other, xr, pt, wcol, (tok,))
    (a1, a2), tok = parts(nt, (2,), True, info, meta, gr, dn, (tok,))
    a_in = both(a1, a2, 0)
    (g_rt, g_lf), tok = parts(nt, (1, -1), False, info, meta, xr, gu, (tok,))
    (g_rt, g_lf), tok = join(g_rt, g_lf, *g_in, (tok,))
    (g_rt, g_lf), tok = gate((g_rt, g_lf), (tok, *a_in))
    g_in = both(g_rt, g_lf, 0)
    (a_rt, a_lf), tok = parts(nt, (1, -1), False, info, meta, gr, dn, (tok,))
    (a_rt, a_lf), tok = join(a_rt, a_lf, *a_in, (tok,))
    a_in = both(a_rt, a_lf, 0)
    (g_own,), tok = parts(nt, (0,), False, info, meta, xr, gu, (tok,))
    (a_own,), tok = parts(nt, (0,), False, info, meta, gr, dn, (tok,))
    (h1, h2, g_rt, g_lf, g_own), tok = turn(g_own, *g_in, (tok,))
    g_in = both(h1, h2, 1)
    (g_rt, g_lf), tok = join_rows(g_rt, g_lf, *g_in, (tok,))
    g_in = both(g_rt, g_lf, 1)
    (h1, h2, a_rt, a_lf, a_own), tok = turn(a_own, *a_in, (tok,))
    a_in = both(h1, h2, 1)
    (gates, ups, act), tok = make_act(r, (g_own, *g_in), (tok,))
    c_in = both(act, act, 1)
    (a_rt, a_lf), tok = join_rows(a_rt, a_lf, *a_in, (tok,))
    a_in = both(a_rt, a_lf, 1)
    (h1, h2), tok = halves(*c_in, (tok,))
    c_far = both(h1, h2, 1)
    delta, tok = make_deltas(r, (gates, ups, wcol, a_own, *a_in), (tok,))
    d_in = both(delta, delta, 1)
    c_line, tok = line(act, c_in[1], c_in[0], *c_far, (tok,))
    c_left, c_right = both(c_line, c_line, 0)
    (h1, h2), tok = halves(*d_in, (tok,))
    d_far = both(h1, h2, 1)
    (h1, h2), tok = halves(c_left, c_right, (tok,))
    c_far = both(h1, h2, 0)
    d_line, tok = line(delta, d_in[1], d_in[0], *d_far, (tok, *c_far))
    d_left, d_right = both(d_line, d_line, 0)

    def back_of(d, bufs, acc, table):
        return back(nt, d, info, meta, bufs, w_gate, w_up, acc, table, (tok,))

    def wgrad_of(d, bufs, prev):
        return wgrad(r, d, info, meta, xe, bufs, prev, (tok,))

    (near, far, act_all), tok = down(nt, info, meta, w_down, wrow, pt, (c_line, c_right, c_left, *c_far), (tok,))
    acc, tok = back_of(0, (d_line,), None, None)
    grads, tok = wgrad_of(0, (d_line,), None)
    mixed_home, tok = to_home(near, far, (tok,))
    (down_grad,), tok = down_grads(r, meta, ge, act_all, (tok,))
    (mixed,), tok = call(mixed_kernel, mixed_home, [VM] * 4, (sds((FEAT, LANE), BF16),), (VM,), after=(tok,))
    (h1, h2), tok = halves(d_left, d_right, (tok,))
    d_far = both(h1, h2, 0)
    acc, tok = back_of(1, (d_right,), acc, None)
    acc, tok = back_of(-1, (d_left,), acc, None)
    grads, tok = wgrad_of(1, (d_right,), grads)
    grads, tok = wgrad_of(-1, (d_left,), grads)
    (near, far), tok = back_of(2, d_far, acc, pt)
    token_home, _ = to_home(near, far, ())
    (gate_grad, up_grad), tok = wgrad_of(2, d_far, grads)
    token_grad, weight_grad = home(*token_home, ids)
    return meta[2], (mixed, token_grad, weight_grad, gate_grad, up_grad, down_grad)


def body(tokens, expert_ids, route_weights, output_grad, w_gate, w_up, w_down):
    info = jnp.stack([lax.axis_index("ctx"), lax.axis_index("exp")]).astype(jnp.int32)
    ids = expert_ids.T
    og = output_grad.T
    weights = (w_gate, w_up, w_down.transpose(0, 2, 1))
    packed = pack(tokens.T, ids, route_weights.T)
    most, outs = passes(5, info, ids, packed, og, *weights)

    def again(state):
        return jnp.zeros_like(state[0]), passes(6, info, ids, packed, og, *weights)[1]

    _, outs = lax.while_loop(lambda state: state[0] > 5, again, (most, outs))
    mixed, token_grad, weight_grad, gate_grad, up_grad, down_grad = outs
    return (
        mixed.T,
        token_grad.T,
        weight_grad.T,
        gate_grad,
        up_grad,
        down_grad.transpose(0, 2, 1),
    )


def solution(mesh):
    return jax.shard_map(
        body,
        mesh=mesh,
        in_specs=(
            P("exp", "ctx"),
            P("exp", None),
            P("exp", None),
            P("exp", "ctx"),
            P("exp", "ctx", None),
            P("exp", "ctx", None),
            P("exp", None, "ctx"),
        ),
        out_specs=(
            P("exp", "ctx"),
            P("exp", "ctx"),
            P("exp", None),
            P("exp", "ctx", None),
            P("exp", "ctx", None),
            P("exp", None, "ctx"),
        ),
        check_vma=False,
    )
```
